32 devices in a mesh: groups: 2 (over y), adapter: 4 (over z), dp: 2 (over x), tensor: 2 (over core).
Axes of the slice: x: 2, y: 2, z: 4, core: 2. Of those that a mesh axis runs over, the one named last changes fastest.
Arguments:
- output_gradient: bfloat16 [4096, 4096], P(('groups', 'dp'), 'tensor'), parts along dimension 0, may hold values from -1.5 to 1.5
- hidden: bfloat16 [4096, 14336], P(('groups', 'dp'), 'adapter'), parts along dimension 0, may hold values from -6 to 6
- frozen_down_weight: bfloat16 [14336, 4096], P('adapter', 'tensor'), may hold values from -0.09375 to 0.09375
- adapter_input_panels: bfloat16 [32, 16, 14336], P(('groups', 'adapter', 'dp')), parts along dimension 0, may hold values from -0.046875 to 0.046875
- adapter_output_panels: bfloat16 [32, 16, 4096], P(('groups', 'adapter', 'dp'), None, 'tensor'), parts along dimension 0, may hold values from -0.09375 to 0.09375
- token_adapter_table: int32 [4096], P('groups'), parts along dimension 0, may hold values from 0 to 15, as said below
- adapter_slot_table: int32 [32], P('groups'), parts along dimension 0, may hold values from 0 to 15, as said below
- segment_live_tokens: int32 [32], P(('groups', 'dp')), parts along dimension 0, may hold values from 32 to 128, as said below
Outputs:
- hidden_gradient: bfloat16 [4096, 14336], P(('groups', 'dp', 'tensor'), 'adapter'), parts along dimension 0
- grad_a: float32 [32, 16, 14336], P(('groups', 'adapter', 'dp'), None, 'tensor'), parts along dimension 0
- grad_b: float32 [32, 16, 4096], P(('groups', 'adapter', 'dp'), None, 'tensor'), parts along dimension 0
The draws below stay inside these ranges and needn't reach their ends.
There are 2 independent parts, one for each index of `groups`. The reference program is written for one: setup_inputs(seed, part) draws one part's arguments, and reference() takes and returns one part's arrays. A program takes and returns all parts, laid end to end along the dimension named above; an argument that names none is the same for every part. Nothing has to cross between parts.
Inputs may be any that keep to these rules, and one draw needn't show every extreme that they name: `token_adapter_table`: within each token block of 1024 tokens (one index of dp) the ids never fall. Counting slots s = adapter_slot_table[id] of the ids that one token block names, no owner block of 2 slots (s // 2) holds more than 1 distinct ones, and in every token block some owner block holds exactly 1. `adapter_slot_table`: A permutation of the slots. `segment_live_tokens`: the tokens past the live ones in a segment are padding. In every token block one segment is full, and in some token block one holds a quarter of 128.
All inputs are finite; a program needn't handle non-finite values.
Results may differ from the reference program's by a relative error of at most 0.0034.
Values may be sent and summed in bfloat16 or wider, within the bound.
A program may use at most 128 MiB of HBM per device.

```python
import jax
import jax.numpy as jnp
from jax import lax

MODEL_WIDTH = 4096
HIDDEN_UNITS = 14336
ADAPTER_RANK = 16
SEG = 128
TOK_DEV = 1024
ADP_DEV = 2
CAP = 1
ADAPTER_SLOTS = 16
TOKENS = 2048


def adapter_layout(key):
    owners = ADAPTER_SLOTS // ADP_DEV
    groups_count = TOKENS // TOK_DEV
    adapter_slot_table = jax.random.permutation(jax.random.fold_in(key, 11), ADAPTER_SLOTS).astype(jnp.int32)
    adapter_of_slot = jnp.argsort(adapter_slot_table, stable=True).astype(jnp.int32)
    counts = jax.random.randint(jax.random.fold_in(key, 12), (groups_count, owners), 0, CAP + 1)
    forced = jax.random.randint(jax.random.fold_in(key, 13), (groups_count,), 0, owners)
    owner_ids = jnp.arange(owners, dtype=jnp.int32)
    counts = jnp.where(owner_ids[None, :] == forced[:, None], CAP, counts)
    scores = jax.random.randint(jax.random.fold_in(key, 14), (groups_count, owners, ADP_DEV), 0, 1 << 20)
    scores = scores * ADP_DEV + jnp.arange(ADP_DEV, dtype=jnp.int32)[None, None, :]
    placing = jnp.argsort(jnp.argsort(scores, axis=2), axis=2).astype(jnp.int32)
    used_flags = (placing < counts[:, :, None]).reshape(groups_count, ADAPTER_SLOTS).astype(jnp.int32)
    running = jnp.cumsum(used_flags, axis=1)
    totals = running[:, -1]
    draws = jax.random.randint(jax.random.fold_in(key, 15), (groups_count, TOK_DEV), 0, 1 << 20) % totals[:, None]
    slot_entries = jnp.sum((running[:, None, :] <= draws[:, :, None]).astype(jnp.int32), axis=2)
    forced_place = jnp.take_along_axis(placing, forced[:, None, None], axis=1)[:, 0, :]
    local_ids = jnp.arange(ADP_DEV, dtype=jnp.int32)
    chosen = jnp.sum(jnp.where(forced_place[:, None, :] == jnp.arange(CAP, dtype=jnp.int32)[None, :, None], local_ids[None, None, :], 0), axis=2)
    forced_slots = forced[:, None] * ADP_DEV + chosen
    slot_entries = slot_entries.at[:, :CAP].set(forced_slots)
    adapter_ids = jnp.sort(adapter_of_slot[slot_entries], axis=1).reshape(TOKENS).astype(jnp.int32)
    return (adapter_slot_table, adapter_ids)


def draw_token_adapter_table(key, part):
    return adapter_layout(key)[1]


def draw_adapter_slot_table(key, part):
    return adapter_layout(key)[0]


def draw_segment_live_tokens(key, part):
    key = jax.random.fold_in(key, 3)
    per_group = TOK_DEV // SEG
    groups_count = TOKENS // TOK_DEV
    values = jax.random.randint(jax.random.fold_in(key, 1), (groups_count, per_group), SEG // 4, SEG + 1)
    first = jax.random.randint(jax.random.fold_in(key, 2), (groups_count,), 0, per_group)
    short_group = jax.random.randint(jax.random.fold_in(key, 4), (), 0, groups_count)
    second = (first + 1) % per_group
    seg_ids = jnp.arange(per_group, dtype=jnp.int32)[None, :]
    group_ids = jnp.arange(groups_count, dtype=jnp.int32)[:, None]
    values = jnp.where(seg_ids == first[:, None], SEG, values)
    values = jnp.where((seg_ids == second[:, None]) & (group_ids == short_group), SEG // 4, values)
    return values.reshape(TOKENS // SEG).astype(jnp.int32)


def steps_of(key, extent, pieces, smallest, top_value):
    level, own = 1.0, jax.random.fold_in(key, 6)
    for axis_at, blocks in pieces:
        heights = jnp.exp(jax.random.uniform(jax.random.fold_in(own, axis_at), (blocks,), jnp.float32, smallest / len(pieces), top_value / len(pieces)))
        level = level * jnp.repeat(heights, extent[axis_at] // blocks).reshape([-1 if axis == axis_at else 1 for axis in range(len(extent))])
    return level


def normal_values(own_key, extent, spread, reach, shards=(), kind=jnp.bfloat16):
    entries = jax.random.normal(own_key, extent, jnp.float32) * spread
    if len(shards) > 0:
        entries = steps_of(own_key, extent, shards, -0.22, 0.18) * entries
    return jnp.clip(entries, min=-reach, max=reach).astype(kind)


def setup_inputs(seed: int = 0, part: int = 0) -> dict:
    key_list = jax.random.split(jax.random.key(seed), 9)
    part_splits = jax.random.split(jax.random.fold_in(key_list[8], part), 9)
    output_gradient = normal_values(part_splits[0], (TOKENS, MODEL_WIDTH), 0.25, 1.5, ((0, 2), (1, 2)))
    hidden = normal_values(part_splits[1], (TOKENS, HIDDEN_UNITS), 1.0, 6.0, ((0, 2), (1, 4)))
    frozen_down_weight = normal_values(key_list[2], (HIDDEN_UNITS, MODEL_WIDTH), MODEL_WIDTH ** -0.5, 0.09375, ((0, 4), (1, 2)))
    adapter_input_panels = normal_values(part_splits[3], (ADAPTER_SLOTS, ADAPTER_RANK, HIDDEN_UNITS), HIDDEN_UNITS ** -0.5, 0.046875, ((0, 8),))
    adapter_output_panels = normal_values(part_splits[4], (ADAPTER_SLOTS, ADAPTER_RANK, MODEL_WIDTH), MODEL_WIDTH ** -0.5, 0.09375, ((0, 8), (2, 2)))
    token_adapter_table = draw_token_adapter_table(jax.random.fold_in(jax.random.fold_in(key_list[8], part), 71), part)
    adapter_slot_table = draw_adapter_slot_table(jax.random.fold_in(jax.random.fold_in(key_list[8], part), 71), part)
    segment_live_tokens = draw_segment_live_tokens(jax.random.fold_in(jax.random.fold_in(key_list[8], part), 71), part)
    return dict(output_gradient=output_gradient, hidden=hidden, frozen_down_weight=frozen_down_weight, adapter_input_panels=adapter_input_panels, adapter_output_panels=adapter_output_panels, token_adapter_table=token_adapter_table, adapter_slot_table=adapter_slot_table, segment_live_tokens=segment_live_tokens)


adapter_scale = 4.0


def reference(output_gradient, hidden, frozen_down_weight, adapter_input_panels, adapter_output_panels, token_adapter_table, adapter_slot_table, segment_live_tokens):
    live_mask = (jnp.arange(SEG, dtype=jnp.int32)[None, :] < segment_live_tokens[:, None]).reshape(TOKENS)
    live_grad = jnp.where(live_mask[:, None], output_gradient, jnp.zeros_like(output_gradient))
    token_slot = jnp.take(adapter_slot_table, token_adapter_table, axis=0).astype(jnp.int32)

    def one_block(carry, index):
        accumulated_down, accumulated_up = carry
        start = (index * SEG).astype(jnp.int32)
        slot_entries = lax.dynamic_slice_in_dim(token_slot, start, SEG, 0)
        hidden_token_rows = lax.dynamic_slice_in_dim(hidden, start, SEG, 0)
        rows_g = lax.dynamic_slice_in_dim(live_grad, start, SEG, 0)
        input_panel = jnp.take(adapter_input_panels, slot_entries, axis=0).astype(jnp.float32)
        output_panel = jnp.take(adapter_output_panels, slot_entries, axis=0).astype(jnp.float32)
        first_round_result = jnp.einsum("ex,emx->em", hidden_token_rows.astype(jnp.float32), input_panel).astype(jnp.bfloat16)
        second_round_result = jnp.einsum("td,trd->tr", rows_g.astype(jnp.float32), output_panel).astype(jnp.bfloat16)
        frozen_rows = jnp.dot(rows_g, frozen_down_weight.T, preferred_element_type=jnp.float32)
        adapter_token_rows = jnp.einsum("kp,kpl->kl", second_round_result.astype(jnp.float32), input_panel)
        gradient_token_rows = (frozen_rows + adapter_scale * adapter_token_rows).astype(jnp.bfloat16)
        outer_input_product = second_round_result.astype(jnp.float32)[:, :, None] * hidden_token_rows.astype(jnp.float32)[:, None, :]
        outer_output_product = first_round_result.astype(jnp.float32)[:, :, None] * rows_g.astype(jnp.float32)[:, None, :]
        accumulated_down = accumulated_down + adapter_scale * jax.ops.segment_sum(outer_input_product, slot_entries, num_segments=ADAPTER_SLOTS)
        accumulated_up = accumulated_up + adapter_scale * jax.ops.segment_sum(outer_output_product, slot_entries, num_segments=ADAPTER_SLOTS)
        return (accumulated_down, accumulated_up), gradient_token_rows

    start_state = (jnp.zeros((ADAPTER_SLOTS, ADAPTER_RANK, HIDDEN_UNITS), jnp.float32), jnp.zeros((ADAPTER_SLOTS, ADAPTER_RANK, MODEL_WIDTH), jnp.float32))
    (grad_a, grad_b), blocks = lax.scan(one_block, start_state, jnp.arange(TOKENS // SEG, dtype=jnp.int32))
    return blocks.reshape(TOKENS, HIDDEN_UNITS), grad_a, grad_b
```

```python
import functools

import jax
import jax.numpy as jnp
from jax import lax
from jax.experimental import pallas as pl
from jax.experimental.pallas import tpu as pltpu
from jax.sharding import PartitionSpec as P

adapter_scale = 4.0
MESH = pl.DeviceIdType.MESH
NT = (((1,), (1,)), ((), ()))
TILE = 256


def lookup(keys_row, table):
    positions = jnp.arange(table.shape[0], dtype=jnp.int32)
    picked = jnp.where(keys_row[:, None] == positions[None, :], table[None, :], 0)
    return jnp.sum(picked, axis=1)


def plain_on_device(
    output_gradient,
    hidden,
    frozen_down_weight,
    adapter_input_panels,
    adapter_output_panels,
    token_adapter_table,
    adapter_slot_table,
    segment_live_tokens,
):
    tok_rows = output_gradient.shape[0]
    half_width = output_gradient.shape[1]
    ff_share = hidden.shape[1]
    owned_slot_list = adapter_input_panels.shape[0]
    rank_extent = adapter_input_panels.shape[1]
    n_adapter = lax.axis_size("adapter")
    n_data = lax.axis_size("dp")
    n_pair = lax.axis_size("tensor")
    capacity = owned_slot_list // 2
    owners = n_adapter * n_data
    n_slots = owners * owned_slot_list
    d_piece = half_width // n_adapter
    ff_piece = ff_share // n_pair
    half_rows = tok_rows // n_pair
    n_recv = owners * capacity
    segment_rows = tok_rows // segment_live_tokens.shape[0]
    at_adapter = lax.axis_index("adapter")
    at_data = lax.axis_index("dp")
    at_pair = lax.axis_index("tensor")
    at_owner = at_adapter * n_data + at_data
    slot_ids = jnp.arange(n_slots, dtype=jnp.int32)
    token_slot = lookup(token_adapter_table, adapter_slot_table).reshape(n_data, tok_rows)
    used_flags = jnp.any(token_slot[:, :, None] == slot_ids[None, None, :], axis=1).astype(
        jnp.int32
    )
    used_blocks = used_flags.reshape(n_data, owners, owned_slot_list)
    order_in_block = jnp.cumsum(used_blocks, axis=2) - 1
    mine_used = lax.dynamic_index_in_dim(used_blocks, at_owner, 1, False)
    mine_order = lax.dynamic_index_in_dim(order_in_block, at_owner, 1, False)
    cap_ids = jnp.arange(capacity, dtype=jnp.int32)
    picks = (mine_used[:, None, :] == 1) & (mine_order[:, None, :] == cap_ids[None, :, None])
    lower_selection = picks.astype(jnp.bfloat16)
    picks_full = picks.astype(jnp.float32)
    sent_a = jnp.einsum(
        "mjt,tou->mjou", lower_selection, adapter_input_panels, preferred_element_type=jnp.float32
    ).astype(jnp.bfloat16)
    sent_b = jnp.einsum(
        "tke,eop->tkop", lower_selection, adapter_output_panels, preferred_element_type=jnp.float32
    ).astype(jnp.bfloat16)
    sent_a = sent_a.reshape(n_data, capacity, rank_extent, n_adapter, ff_share).transpose(
        3, 0, 1, 2, 4
    )
    sent_b = sent_b.reshape(n_data, capacity, rank_extent, n_adapter, d_piece).transpose(
        3, 0, 1, 2, 4
    )
    flat_a = sent_a.reshape(n_recv, rank_extent, ff_share)
    flat_b = sent_b.reshape(n_recv, rank_extent, d_piece)
    got_a, got_b = (
        lax.all_to_all(flat_a, ("adapter", "dp"), split_axis=0, concat_axis=0, tiled=True),
        lax.all_to_all(flat_b, ("adapter", "dp"), split_axis=0, concat_axis=0, tiled=True),
    )
    panels_a = got_a.reshape(n_recv * rank_extent, ff_share)
    panels_b = got_b.reshape(n_recv * rank_extent, d_piece)
    my_slots = lax.dynamic_index_in_dim(token_slot, at_data, 0, False)
    my_order = lax.dynamic_index_in_dim(order_in_block, at_data, 0, False).reshape(n_slots)
    recv_index = my_slots // owned_slot_list * capacity + lookup(my_slots, my_order)
    recv_ids = jnp.arange(n_recv, dtype=jnp.int32)
    select = (recv_index[:, None] == recv_ids[None, :])[:, :, None]
    seg_pos = jnp.arange(segment_rows, dtype=jnp.int32)
    live_mask = (seg_pos[None, :] < segment_live_tokens[:, None]).reshape(tok_rows)
    live_grad = jnp.where(live_mask[:, None], output_gradient, jnp.zeros_like(output_gradient))
    hidden_part = lax.dynamic_slice_in_dim(hidden, at_pair * ff_piece, ff_piece, 1)
    panels_part = lax.dynamic_slice_in_dim(panels_a, at_pair * ff_piece, ff_piece, 1)
    grad_piece = lax.dynamic_slice_in_dim(live_grad, at_adapter * d_piece, d_piece, 1)
    wide_u = jnp.einsum("tf,kf->tk", hidden_part, panels_part, preferred_element_type=jnp.float32)
    wide_v = jnp.einsum("td,kd->tk", grad_piece, panels_b, preferred_element_type=jnp.float32)
    part_u = jnp.sum(jnp.where(select, wide_u.reshape(tok_rows, n_recv, rank_extent), 0.0), axis=1)
    part_v = jnp.sum(jnp.where(select, wide_v.reshape(tok_rows, n_recv, rank_extent), 0.0), axis=1)
    full_u, full_v = lax.psum((part_u, part_v), ("adapter", "tensor"))
    first_round_result = full_u.astype(jnp.bfloat16)
    second_round_result = full_v.astype(jnp.bfloat16)
    zero_low = jnp.zeros((), jnp.bfloat16)
    spread_u = jnp.where(select, first_round_result[:, None, :], zero_low).reshape(
        tok_rows, n_recv * rank_extent
    )
    spread_v = jnp.where(select, second_round_result[:, None, :], zero_low).reshape(
        tok_rows, n_recv * rank_extent
    )
    frozen_portion = lax.psum_scatter(
        jnp.einsum("td,fd->tf", live_grad, frozen_down_weight, preferred_element_type=jnp.float32),
        "tensor",
        scatter_dimension=0,
        tiled=True,
    )
    spread_half = lax.dynamic_slice_in_dim(spread_v, at_pair * half_rows, half_rows, 0)
    hidden_half = lax.dynamic_slice_in_dim(hidden, at_pair * half_rows, half_rows, 0)
    adapter_token_rows = jnp.dot(spread_half, panels_a, preferred_element_type=jnp.float32)
    hidden_gradient = (frozen_portion + adapter_scale * adapter_token_rows).astype(jnp.bfloat16)
    input_portion = adapter_scale * jnp.einsum(
        "tk,tf->kf", spread_half, hidden_half, preferred_element_type=jnp.float32
    )
    output_portion = adapter_scale * jnp.einsum(
        "tk,td->kd", spread_u, grad_piece, preferred_element_type=jnp.float32
    )
    a_width = input_portion.shape[1]
    back_a = input_portion.reshape(n_adapter, n_data, capacity, rank_extent, a_width)
    back_b = output_portion.reshape(n_adapter, n_data, capacity, rank_extent, d_piece)
    flat_back_a = back_a.reshape(n_recv, rank_extent, a_width)
    flat_back_b = back_b.reshape(n_recv, rank_extent, d_piece)
    ret_a, ret_b = (
        lax.all_to_all(flat_back_a, ("adapter", "dp"), split_axis=0, concat_axis=0, tiled=True),
        lax.all_to_all(flat_back_b, ("adapter", "dp"), split_axis=0, concat_axis=0, tiled=True),
    )
    ret_a = ret_a.reshape(n_adapter, n_data, capacity, rank_extent, a_width)
    ret_b = ret_b.reshape(n_adapter, n_data, capacity, rank_extent, d_piece)
    own_a = jnp.einsum("jcl,kjcrf->lrkf", picks_full, ret_a, precision=lax.Precision.HIGHEST)
    own_b = jnp.einsum("jcl,kjcrd->lrkd", picks_full, ret_b, precision=lax.Precision.HIGHEST)
    own_b = own_b.reshape(owned_slot_list, rank_extent, half_width)
    own_a = own_a.reshape(owned_slot_list, rank_extent, n_adapter * a_width)
    grad_a = lax.psum_scatter(own_a, "tensor", scatter_dimension=2, tiled=True)
    return (hidden_gradient, grad_a, own_b)


def fused_kernel(
    sizes,
    grad_hbm,
    hidden_hbm,
    weight_hbm,
    sent_a_hbm,
    sent_b_hbm,
    choose_ref,
    choose_mine_ref,
    live_ref,
    pick_ref,
    out_hbm,
    grad_a_ref,
    grad_b_ref,
    grad,
    hid,
    weight,
    panels_a,
    panels_b,
    own_acc,
    to_pair,
    from_pair,
    staged,
    part,
    part_in,
    low,
    spread,
    spread_own,
    piece_a,
    back_a,
    piece_b,
    back_b,
    load_sem,
    weight_sem,
    out_sem,
    a_send,
    a_recv,
    b_send,
    b_recv,
    pair_send,
    pair_recv,
    fwd_sem,
    rs_send,
    rs_recv,
    ag_send,
    ag_recv,
    ra_send,
    ra_recv,
    rb_send,
    rb_recv,
):
    n_adapter, n_data, n_pair, rank = sizes
    tok, width = grad.shape
    half = tok // n_pair
    ff_half = hid.shape[1]
    ff = ff_half * n_pair
    n_own = n_adapter * n_data
    n_sum = n_adapter * n_pair
    tok_piece = tok // n_sum
    n_tile = ff // TILE
    at_g = lax.axis_index("groups")
    at_a = lax.axis_index("adapter")
    at_d = lax.axis_index("dp")
    at_t = lax.axis_index("tensor")
    at_own = at_a * n_data + at_d
    at_sum = at_a * n_pair + at_t

    def dev(a, d, t):
        return (at_g, a, d, t)

    def remote(src, dst, send, recv, to):
        return pltpu.make_async_remote_copy(
            src_ref=src, dst_ref=dst, send_sem=send, recv_sem=recv, device_id=to, device_id_type=MESH
        )

    def lanes(start, size):
        return pl.ds(pl.multiple_of(start, 128), size)

    def rows(start, size):
        return pl.ds(pl.multiple_of(start, 16), size)

    load_grad = pltpu.make_async_copy(grad_hbm, grad, load_sem.at[0])
    load_hid = pltpu.make_async_copy(
        hidden_hbm.at[:, lanes(at_t * ff_half, ff_half)], hid, load_sem.at[1]
    )
    load_grad.start()

    def load_weight(c):
        place = pl.ds(pl.multiple_of(c * TILE, TILE), TILE)
        return pltpu.make_async_copy(weight_hbm.at[place, :], weight.at[place, :], weight_sem.at[c])

    def start_weight(c, _):
        load_weight(c).start()
        return 0

    load_weight(0).start()
    load_weight(1).start()

    at_all = at_own * n_pair + at_t
    n_all = n_own * n_pair
    barrier = pltpu.get_barrier_semaphore()

    def greet(k, _):
        i = lax.rem(at_all + k, n_all)
        pl.semaphore_signal(
            barrier,
            inc=1,
            device_id=dev(
                lax.div(i, n_data * n_pair), lax.rem(lax.div(i, n_pair), n_data), lax.rem(i, n_pair)
            ),
            device_id_type=MESH,
        )
        return 0

    lax.fori_loop(1, n_all, greet, 0)
    pl.semaphore_wait(barrier, n_all - 1)

    b_copies = [
        pltpu.make_async_copy(
            sent_b_hbm.at[at_d], panels_b.at[rows(at_d * rank, rank), :], load_sem.at[2]
        )
    ]
    for k in range(1, n_data):
        j = lax.rem(at_d + k, n_data)
        b_copies.append(
            remote(
                sent_b_hbm.at[j],
                panels_b.at[rows(at_d * rank, rank), :],
                b_send.at[k],
                b_recv.at[k],
                dev(at_a, j, at_t),
            )
        )
    for copy in b_copies:
        copy.start()

    mine = lanes(at_t * ff_half, ff_half)
    a_copies = [
        pltpu.make_async_copy(
            sent_a_hbm.at[at_d, :, lanes(at_a * ff + at_t * ff_half, ff_half)],
            panels_a.at[rows(at_own * rank, rank), mine],
            load_sem.at[3],
        )
    ]
    for k in range(1, n_own):
        o = lax.rem(at_own + k, n_own)
        a2, d2 = lax.div(o, n_data), lax.rem(o, n_data)
        a_copies.append(
            remote(
                sent_a_hbm.at[d2, :, lanes(a2 * ff + at_t * ff_half, ff_half)],
                panels_a.at[rows(at_own * rank, rank), mine],
                a_send.at[k],
                a_recv.at[k],
                dev(a2, d2, at_t),
            )
        )
    for copy in a_copies:
        copy.start()
    lax.fori_loop(2, 6, start_weight, 0)
    load_hid.start()
    lax.fori_loop(6, n_tile, start_weight, 0)
    load_grad.wait()

    pair_dev = dev(at_a, at_d, 1 - at_t)
    mine_rows = pl.ds(pl.multiple_of(at_t * half, half), half)
    pair_rows = pl.ds(pl.multiple_of((1 - at_t) * half, half), half)

    def pair_copy(c):
        return remote(to_pair.at[c], from_pair.at[c], pair_send.at[c], pair_recv.at[c], pair_dev)

    forward = remote(
        panels_a.at[:, mine], panels_a.at[:, mine], fwd_sem.at[0], fwd_sem.at[1], pair_dev
    )

    def sum_peer(k):
        q = lax.rem(at_sum + k, n_sum)
        return q, dev(lax.div(q, n_pair), at_d, lax.rem(q, n_pair))

    def scatter_copies(w):
        copies = []
        for k in range(1, n_sum):
            q, to = sum_peer(k)
            copies.append(
                remote(
                    part.at[w, q], part_in.at[w, k], rs_send.at[w, k], rs_recv.at[w, k], to
                )
            )
        return copies

    def gather_copies(w):
        copies = []
        for k in range(1, n_sum):
            _, to = sum_peer(k)
            copies.append(
                remote(
                    low.at[w, at_sum], low.at[w, at_sum], ag_send.at[w, k], ag_recv.at[w, k], to
                )
            )
        return copies

    def start_all(copies):
        for copy in copies:
            copy.start()

    def wait_all(copies):
        for copy in copies:
            copy.wait()

    def store_part(w, i, value):
        for s in range(TILE // tok_piece):
            part[w, i * (TILE // tok_piece) + s] = value[:, s * tok_piece : (s + 1) * tok_piece]

    def part_v():
        wait_all(b_copies)

        def step(i, _):
            block = grad[pl.ds(pl.multiple_of(i * TILE, TILE), TILE), :]
            wide = lax.dot_general(panels_b[...], block, NT, preferred_element_type=jnp.float32)
            total = jnp.zeros((rank, TILE), jnp.float32)
            for j in range(n_data):
                keep = choose_mine_ref[j : j + 1, lanes(i * TILE, TILE)]
                total += wide[j * rank : (j + 1) * rank] * keep
            store_part(1, i, total)
            return 0

        lax.fori_loop(0, tok // TILE, step, 0)
        start_all(scatter_copies(1))

    def part_u():
        wait_all(a_copies)
        forward.start()

        def step(i, _):
            block = hid[pl.ds(pl.multiple_of(i * TILE, TILE), TILE), :]
            wide = lax.dot_general(
                panels_a[:, mine], block, NT, preferred_element_type=jnp.float32
            )
            total = jnp.zeros((rank, TILE), jnp.float32)
            for o in range(n_own):
                keep = choose_ref[o : o + 1, lanes(i * TILE, TILE)]
                total += wide[o * rank : (o + 1) * rank] * keep
            store_part(0, i, total)
            return 0

        lax.fori_loop(0, tok // TILE, step, 0)
        start_all(scatter_copies(0))

    def sum_low(w):
        wait_all(scatter_copies(w))
        total = part[w, at_sum]
        for k in range(1, n_sum):
            total += part_in[w, k]
        low[w, at_sum] = total.astype(jnp.bfloat16)
        start_all(gather_copies(w))

    def use_v():
        wait_all(gather_copies(1))
        for i in range(n_sum):
            value = low[1, i].astype(jnp.float32) * adapter_scale
            place = slice(i * tok_piece, (i + 1) * tok_piece)
            for o in range(n_own):
                spread[o * rank : (o + 1) * rank, place] = (
                    value * choose_ref[o : o + 1, place]
                ).astype(jnp.bfloat16)
        load_hid.wait()

        def step(i, _):
            place = lanes(i * TILE, TILE)
            piece_a[:, place] = jnp.dot(
                spread[...], hid[:, place], preferred_element_type=jnp.float32
            ).astype(jnp.bfloat16)
            return 0

        lax.fori_loop(0, ff_half // TILE, step, 0)
        spread_own[...] = jnp.transpose(
            spread[:, lanes(at_t * half, half)].astype(jnp.float32)
        ).astype(jnp.bfloat16)
        return_a(True)

    ratio = n_adapter // n_pair
    core = lax.div(at_a, ratio)
    low_a = lax.rem(at_a, ratio)
    ret_slot = (low_a * n_data + at_d) * n_pair + at_t
    ret_place = lanes(low_a * ff + at_t * ff_half, ff_half)

    def return_copy(k):
        o = lax.rem(at_own + k, n_own)
        return remote(
            piece_a.at[rows(o * rank, rank), :],
            back_a.at[at_d, :, ret_place],
            ra_send.at[k],
            ra_recv.at[ret_slot],
            dev(lax.div(o, n_data), lax.rem(o, n_data), core),
        )

    def return_a(start):
        for k in range(1, n_own):
            if start:
                return_copy(k).start()
            else:
                return_copy(k).wait_send()

        @pl.when(at_t != core)
        def _():
            if start:
                return_copy(0).start()
            else:
                return_copy(0).wait_send()

        if start:

            @pl.when(at_t == core)
            def _():
                pltpu.make_async_copy(
                    piece_a.at[rows(at_own * rank, rank), :],
                    back_a.at[at_d, :, ret_place],
                    ra_recv.at[ret_slot],
                ).start()

    def wait_returned():
        for s in range(ratio * n_data * n_pair):
            a2, d2, t2 = s // (n_data * n_pair), s // n_pair % n_data, s % n_pair
            first = a2 * ff + t2 * ff_half
            place = back_a.at[d2, :, first : first + ff_half]
            remote(place, place, ra_send.at[0], ra_recv.at[s], pair_dev).wait_recv()

    def return_b():
        copies = []
        for k in range(1, n_data):
            j = lax.rem(at_d + k, n_data)
            copies.append(
                remote(
                    piece_b.at[j], back_b.at[k], rb_send.at[k], rb_recv.at[k], dev(at_a, j, at_t)
                )
            )
        return copies

    def use_u():
        wait_all(gather_copies(0))
        parts = []
        for i in range(n_sum):
            value = low[0, i].astype(jnp.float32) * adapter_scale
            place = slice(i * tok_piece, (i + 1) * tok_piece)
            parts.append(
                jnp.concatenate(
                    [
                        value * choose_mine_ref[j : j + 1, place]
                        for j in range(n_data)
                    ],
                    axis=0,
                ).astype(jnp.bfloat16)
            )
        spread_u = jnp.concatenate(parts, axis=1)
        for i in range(width // 512):
            place = slice(i * 512, (i + 1) * 512)
            wide = jnp.dot(spread_u, grad[:, place], preferred_element_type=jnp.float32)
            for j in range(n_data):
                piece_b[j, :, place] = wide[j * rank : (j + 1) * rank]
        start_all(return_b())

    events = {
        1: part_v,
        3: lambda: sum_low(1),
        5: use_v,
        7: part_u,
        9: lambda: sum_low(0),
        11: use_u,
    }

    def main(c, _):
        load_weight(c).wait()
        w = weight[pl.ds(pl.multiple_of(c * TILE, TILE), TILE), :]
        to_pair[c] = lax.dot_general(
            grad[pair_rows, :], w, NT, preferred_element_type=jnp.float32
        ).astype(jnp.bfloat16)
        pair_copy(c).start()
        own_acc[c] = lax.dot_general(grad[mine_rows, :], w, NT, preferred_element_type=jnp.float32)
        for at, event in events.items():
            pl.when(c == min(at, n_tile - 1))(event)
        return 0

    lax.fori_loop(0, n_tile, main, 0)
    forward.wait()

    def store_copy(c):
        return pltpu.make_async_copy(staged.at[c], out_hbm.at[:, lanes(c * TILE, TILE)], out_sem.at[c])

    def finish(c, _):
        pair_copy(c).wait()
        total = own_acc[c] + from_pair[c].astype(jnp.float32)
        total += jnp.dot(
            spread_own[...], panels_a[:, lanes(c * TILE, TILE)], preferred_element_type=jnp.float32
        )
        staged[c] = jnp.where(live_ref[...] > 0, total, 0.0).astype(jnp.bfloat16)
        store_copy(c).start()
        return 0

    lax.fori_loop(0, n_tile, finish, 0)

    wait_all(return_b())
    n_slot = grad_b_ref.shape[0]
    for l in range(n_slot):
        total = piece_b[at_d] * pick_ref[at_d, l]
        for k in range(1, n_data):
            total += back_b[k] * pick_ref[lax.rem(at_d + n_data - k, n_data), l]
        grad_b_ref[l] = total
    return_a(False)
    wait_returned()
    for l in range(n_slot):
        total = back_a[0].astype(jnp.float32) * pick_ref[0, l]
        for d in range(1, n_data):
            total += back_a[d].astype(jnp.float32) * pick_ref[d, l]
        grad_a_ref[l] = total

    def drain(c, _):
        store_copy(c).wait()
        return 0

    lax.fori_loop(0, n_tile, drain, 0)


def fused_on_device(
    output_gradient,
    hidden,
    frozen_down_weight,
    adapter_input_panels,
    adapter_output_panels,
    token_adapter_table,
    adapter_slot_table,
    segment_live_tokens,
):
    tok, width = output_gradient.shape
    ff = hidden.shape[1]
    n_slot, rank, ff_all = adapter_input_panels.shape
    n_adapter = lax.axis_size("adapter")
    n_data = lax.axis_size("dp")
    n_pair = lax.axis_size("tensor")
    n_own = n_adapter * n_data
    n_sum = n_adapter * n_pair
    half = tok // n_pair
    ff_half = ff // n_pair
    n_tile = ff // TILE
    at_data = lax.axis_index("dp")
    at_pair = lax.axis_index("tensor")
    at_own = lax.axis_index("adapter") * n_data + at_data
    token_slot = lookup(token_adapter_table, adapter_slot_table).reshape(n_data, tok)
    my_ids = at_own * n_slot + jnp.arange(n_slot, dtype=jnp.int32)
    pick = jnp.any(token_slot[:, :, None] == my_ids[None, None, :], axis=1)
    sent_a = jnp.zeros((n_data, rank, ff_all), jnp.bfloat16)
    sent_b = jnp.zeros((n_data, rank, width), jnp.bfloat16)
    for l in range(n_slot):
        sent_a = jnp.where(pick[:, l, None, None], adapter_input_panels[l][None], sent_a)
        sent_b = jnp.where(pick[:, l, None, None], adapter_output_panels[l][None], sent_b)
    seg = tok // segment_live_tokens.shape[0]
    seg_pos = jnp.arange(seg, dtype=jnp.int32)
    live = (seg_pos[None, :] < segment_live_tokens[:, None]).reshape(tok)
    my_owner = lax.dynamic_index_in_dim(token_slot, at_data, 0, False) // n_slot
    owner_ids = jnp.arange(n_own, dtype=jnp.int32)
    choose = ((my_owner[None, :] == owner_ids[:, None]) & live[None, :]).astype(jnp.float32)
    choose_mine = lax.dynamic_slice_in_dim(choose, at_own - at_data, n_data, 0)
    live_half = lax.dynamic_slice_in_dim(live, at_pair * half, half, 0).astype(jnp.float32)[:, None]
    anywhere = pl.BlockSpec(memory_space=pl.ANY)
    vmem = pl.BlockSpec(memory_space=pltpu.VMEM)
    dma = pltpu.SemaphoreType.DMA
    bf16, f32 = jnp.bfloat16, jnp.float32
    ff_out = ff_all // n_pair
    n_back = n_adapter // n_pair * n_data * n_pair
    return pl.pallas_call(
        functools.partial(fused_kernel, (n_adapter, n_data, n_pair, rank)),
        out_shape=(
            jax.ShapeDtypeStruct((half, ff), bf16),
            jax.ShapeDtypeStruct((n_slot, rank, ff_out), f32),
            jax.ShapeDtypeStruct((n_slot, rank, width), f32),
        ),
        in_specs=[anywhere] * 5 + [vmem, vmem, vmem, pl.BlockSpec(memory_space=pltpu.SMEM)],
        out_specs=(anywhere, vmem, vmem),
        scratch_shapes=[
            pltpu.VMEM((tok, width), bf16),
            pltpu.VMEM((tok, ff_half), bf16),
            pltpu.VMEM((ff, width), bf16),
            pltpu.VMEM((n_own * rank, ff), bf16),
            pltpu.VMEM((n_data * rank, width), bf16),
            pltpu.VMEM((n_tile, half, TILE), f32),
            pltpu.VMEM((n_tile, half, TILE), bf16),
            pltpu.VMEM((n_tile, half, TILE), bf16),
            pltpu.VMEM((n_tile, half, TILE), bf16),
            pltpu.VMEM((2, n_sum, rank, tok // n_sum), f32),
            pltpu.VMEM((2, n_sum, rank, tok // n_sum), f32),
            pltpu.VMEM((2, n_sum, rank, tok // n_sum), bf16),
            pltpu.VMEM((n_own * rank, tok), bf16),
            pltpu.VMEM((half, n_own * rank), bf16),
            pltpu.VMEM((n_own * rank, ff_half), bf16),
            pltpu.VMEM((n_data, rank, ff_out), bf16),
            pltpu.VMEM((n_data, rank, width), f32),
            pltpu.VMEM((n_data, rank, width), f32),
            dma((4,)),
            dma((n_tile,)),
            dma((n_tile,)),
            dma((n_own,)),
            dma((n_own,)),
            dma((n_data,)),
            dma((n_data,)),
            dma((n_tile,)),
            dma((n_tile,)),
            dma((2,)),
            dma((2, n_sum)),
            dma((2, n_sum)),
            dma((2, n_sum)),
            dma((2, n_sum)),
            dma((n_own,)),
            dma((n_back,)),
            dma((n_data,)),
            dma((n_data,)),
        ],
        compiler_params=pltpu.CompilerParams(
            collective_id=0, has_side_effects=True, vmem_limit_bytes=60 * 1024 * 1024
        ),
        cost_estimate=pl.CostEstimate(
            flops=2 * tok * width * ff, bytes_accessed=2 * ff * width, transcendentals=0
        ),
    )(
        output_gradient,
        hidden,
        frozen_down_weight,
        sent_a,
        sent_b,
        choose,
        choose_mine,
        live_half,
        pick.astype(jnp.float32),
    )


def fits_kernel(hidden, adapter_input_panels):
    ff = hidden.shape[1]
    n_slot, rank, _ = adapter_input_panels.shape
    n_adapter = lax.axis_size("adapter")
    n_data = lax.axis_size("dp")
    n_pair = lax.axis_size("tensor")
    n_sum = n_adapter * n_pair
    return (
        n_pair == 2
        and n_slot == 2
        and rank == 16
        and n_adapter % n_pair == 0
        and ff % (n_pair * TILE) == 0
        and ff // TILE > 11
        and hidden.shape[0] == n_sum * 128
        and n_adapter * n_data * rank <= 256
    )


def on_device(*args):
    if fits_kernel(args[1], args[3]):
        return fused_on_device(*args)
    return plain_on_device(*args)


def solution(mesh):
    placed = (
        P(("groups", "dp"), "tensor"),
        P(("groups", "dp"), "adapter"),
        P("adapter", "tensor"),
        P(("groups", "adapter", "dp"), None, None),
        P(("groups", "adapter", "dp"), None, "tensor"),
        P("groups"),
        P("groups"),
        P(("groups", "dp")),
    )
    return jax.shard_map(
        on_device,
        mesh=mesh,
        in_specs=placed,
        out_specs=(
            P(("groups", "dp", "tensor"), "adapter"),
            P(("groups", "adapter", "dp"), None, "tensor"),
            P(("groups", "adapter", "dp"), None, "tensor"),
        ),
        check_vma=False,
    )
```

```python
import functools

import jax
import jax.numpy as jnp
from jax import lax
from jax.experimental import pallas as pl
from jax.experimental.pallas import tpu as pltpu
from jax.sharding import PartitionSpec as P

adapter_scale = 4.0
MESH = pl.DeviceIdType.MESH
NT = (((1,), (1,)), ((), ()))
TILE = 256


def lookup(keys_row, table):
    positions = jnp.arange(table.shape[0], dtype=jnp.int32)
    picked = jnp.where(keys_row[:, None] == positions[None, :], table[None, :], 0)
    return jnp.sum(picked, axis=1)


def plain_on_device(
    output_gradient,
    hidden,
    frozen_down_weight,
    adapter_input_panels,
    adapter_output_panels,
    token_adapter_table,
    adapter_slot_table,
    segment_live_tokens,
):
    tok_rows = output_gradient.shape[0]
    half_width = output_gradient.shape[1]
    ff_share = hidden.shape[1]
    owned_slot_list = adapter_input_panels.shape[0]
    rank_extent = adapter_input_panels.shape[1]
    n_adapter = lax.axis_size("adapter")
    n_data = lax.axis_size("dp")
    n_pair = lax.axis_size("tensor")
    capacity = owned_slot_list // 2
    owners = n_adapter * n_data
    n_slots = owners * owned_slot_list
    d_piece = half_width // n_adapter
    ff_piece = ff_share // n_pair
    half_rows = tok_rows // n_pair
    n_recv = owners * capacity
    segment_rows = tok_rows // segment_live_tokens.shape[0]
    at_adapter = lax.axis_index("adapter")
    at_data = lax.axis_index("dp")
    at_pair = lax.axis_index("tensor")
    at_owner = at_adapter * n_data + at_data
    slot_ids = jnp.arange(n_slots, dtype=jnp.int32)
    token_slot = lookup(token_adapter_table, adapter_slot_table).reshape(n_data, tok_rows)
    used_flags = jnp.any(token_slot[:, :, None] == slot_ids[None, None, :], axis=1).astype(
        jnp.int32
    )
    used_blocks = used_flags.reshape(n_data, owners, owned_slot_list)
    order_in_block = jnp.cumsum(used_blocks, axis=2) - 1
    mine_used = lax.dynamic_index_in_dim(used_blocks, at_owner, 1, False)
    mine_order = lax.dynamic_index_in_dim(order_in_block, at_owner, 1, False)
    cap_ids = jnp.arange(capacity, dtype=jnp.int32)
    picks = (mine_used[:, None, :] == 1) & (mine_order[:, None, :] == cap_ids[None, :, None])
    lower_selection = picks.astype(jnp.bfloat16)
    picks_full = picks.astype(jnp.float32)
    sent_a = jnp.einsum(
        "mjt,tou->mjou", lower_selection, adapter_input_panels, preferred_element_type=jnp.float32
    ).astype(jnp.bfloat16)
    sent_b = jnp.einsum(
        "tke,eop->tkop", lower_selection, adapter_output_panels, preferred_element_type=jnp.float32
    ).astype(jnp.bfloat16)
    sent_a = sent_a.reshape(n_data, capacity, rank_extent, n_adapter, ff_share).transpose(
        3, 0, 1, 2, 4
    )
    sent_b = sent_b.reshape(n_data, capacity, rank_extent, n_adapter, d_piece).transpose(
        3, 0, 1, 2, 4
    )
    flat_a = sent_a.reshape(n_recv, rank_extent, ff_share)
    flat_b = sent_b.reshape(n_recv, rank_extent, d_piece)
    got_a, got_b = (
        lax.all_to_all(flat_a, ("adapter", "dp"), split_axis=0, concat_axis=0, tiled=True),
        lax.all_to_all(flat_b, ("adapter", "dp"), split_axis=0, concat_axis=0, tiled=True),
    )
    panels_a = got_a.reshape(n_recv * rank_extent, ff_share)
    panels_b = got_b.reshape(n_recv * rank_extent, d_piece)
    my_slots = lax.dynamic_index_in_dim(token_slot, at_data, 0, False)
    my_order = lax.dynamic_index_in_dim(order_in_block, at_data, 0, False).reshape(n_slots)
    recv_index = my_slots // owned_slot_list * capacity + lookup(my_slots, my_order)
    recv_ids = jnp.arange(n_recv, dtype=jnp.int32)
    select = (recv_index[:, None] == recv_ids[None, :])[:, :, None]
    seg_pos = jnp.arange(segment_rows, dtype=jnp.int32)
    live_mask = (seg_pos[None, :] < segment_live_tokens[:, None]).reshape(tok_rows)
    live_grad = jnp.where(live_mask[:, None], output_gradient, jnp.zeros_like(output_gradient))
    hidden_part = lax.dynamic_slice_in_dim(hidden, at_pair * ff_piece, ff_piece, 1)
    panels_part = lax.dynamic_slice_in_dim(panels_a, at_pair * ff_piece, ff_piece, 1)
    grad_piece = lax.dynamic_slice_in_dim(live_grad, at_adapter * d_piece, d_piece, 1)
    wide_u = jnp.einsum("tf,kf->tk", hidden_part, panels_part, preferred_element_type=jnp.float32)
    wide_v = jnp.einsum("td,kd->tk", grad_piece, panels_b, preferred_element_type=jnp.float32)
    part_u = jnp.sum(jnp.where(select, wide_u.reshape(tok_rows, n_recv, rank_extent), 0.0), axis=1)
    part_v = jnp.sum(jnp.where(select, wide_v.reshape(tok_rows, n_recv, rank_extent), 0.0), axis=1)
    full_u, full_v = lax.psum((part_u, part_v), ("adapter", "tensor"))
    first_round_result = full_u.astype(jnp.bfloat16)
    second_round_result = full_v.astype(jnp.bfloat16)
    zero_low = jnp.zeros((), jnp.bfloat16)
    spread_u = jnp.where(select, first_round_result[:, None, :], zero_low).reshape(
        tok_rows, n_recv * rank_extent
    )
    spread_v = jnp.where(select, second_round_result[:, None, :], zero_low).reshape(
        tok_rows, n_recv * rank_extent
    )
    frozen_portion = lax.psum_scatter(
        jnp.einsum("td,fd->tf", live_grad, frozen_down_weight, preferred_element_type=jnp.float32),
        "tensor",
        scatter_dimension=0,
        tiled=True,
    )
    spread_half = lax.dynamic_slice_in_dim(spread_v, at_pair * half_rows, half_rows, 0)
    hidden_half = lax.dynamic_slice_in_dim(hidden, at_pair * half_rows, half_rows, 0)
    adapter_token_rows = jnp.dot(spread_half, panels_a, preferred_element_type=jnp.float32)
    hidden_gradient = (frozen_portion + adapter_scale * adapter_token_rows).astype(jnp.bfloat16)
    input_portion = adapter_scale * jnp.einsum(
        "tk,tf->kf", spread_half, hidden_half, preferred_element_type=jnp.float32
    )
    output_portion = adapter_scale * jnp.einsum(
        "tk,td->kd", spread_u, grad_piece, preferred_element_type=jnp.float32
    )
    a_width = input_portion.shape[1]
    back_a = input_portion.reshape(n_adapter, n_data, capacity, rank_extent, a_width)
    back_b = output_portion.reshape(n_adapter, n_data, capacity, rank_extent, d_piece)
    flat_back_a = back_a.reshape(n_recv, rank_extent, a_width)
    flat_back_b = back_b.reshape(n_recv, rank_extent, d_piece)
    ret_a, ret_b = (
        lax.all_to_all(flat_back_a, ("adapter", "dp"), split_axis=0, concat_axis=0, tiled=True),
        lax.all_to_all(flat_back_b, ("adapter", "dp"), split_axis=0, concat_axis=0, tiled=True),
    )
    ret_a = ret_a.reshape(n_adapter, n_data, capacity, rank_extent, a_width)
    ret_b = ret_b.reshape(n_adapter, n_data, capacity, rank_extent, d_piece)
    own_a = jnp.einsum("jcl,kjcrf->lrkf", picks_full, ret_a, precision=lax.Precision.HIGHEST)
    own_b = jnp.einsum("jcl,kjcrd->lrkd", picks_full, ret_b, precision=lax.Precision.HIGHEST)
    own_b = own_b.reshape(owned_slot_list, rank_extent, half_width)
    own_a = own_a.reshape(owned_slot_list, rank_extent, n_adapter * a_width)
    grad_a = lax.psum_scatter(own_a, "tensor", scatter_dimension=2, tiled=True)
    return (hidden_gradient, grad_a, own_b)


def fused_kernel(
    sizes,
    grad_hbm,
    hidden_hbm,
    weight_hbm,
    slots_a_hbm,
    slots_b_hbm,
    ids_ref,
    table_ref,
    seg_ref,
    out_hbm,
    grad_a_ref,
    grad_b_ref,
    grad,
    hid,
    weight,
    slots_a,
    slots_b,
    sent_a,
    sent_b,
    choose_ref,
    choose_mine_ref,
    live_ref,
    panels_a,
    panels_b,
    own_acc,
    to_pair,
    from_pair,
    staged,
    part,
    part_in,
    low,
    spread,
    spread_own,
    piece_a,
    back_a,
    piece_b,
    back_b,
    load_sem,
    weight_sem,
    out_sem,
    a_send,
    a_recv,
    b_send,
    b_recv,
    pair_send,
    pair_recv,
    fwd_sem,
    rs_send,
    rs_recv,
    ag_send,
    ag_recv,
    ra_send,
    ra_recv,
    rb_send,
    rb_recv,
):
    n_adapter, n_data, n_pair, rank = sizes
    tok, width = grad.shape
    half = tok // n_pair
    ff_half = hid.shape[1]
    ff = ff_half * n_pair
    n_own = n_adapter * n_data
    n_sum = n_adapter * n_pair
    tok_piece = tok // n_sum
    n_tile = ff // TILE
    at_g = lax.axis_index("groups")
    at_a = lax.axis_index("adapter")
    at_d = lax.axis_index("dp")
    at_t = lax.axis_index("tensor")
    at_own = at_a * n_data + at_d
    at_sum = at_a * n_pair + at_t

    def dev(a, d, t):
        return (at_g, a, d, t)

    def remote(src, dst, send, recv, to):
        return pltpu.make_async_remote_copy(
            src_ref=src, dst_ref=dst, send_sem=send, recv_sem=recv, device_id=to, device_id_type=MESH
        )

    def lanes(start, size):
        return pl.ds(pl.multiple_of(start, 128), size)

    def rows(start, size):
        return pl.ds(pl.multiple_of(start, 16), size)

    load_grad = pltpu.make_async_copy(grad_hbm, grad, load_sem.at[0])
    load_hid = pltpu.make_async_copy(
        hidden_hbm.at[:, lanes(at_t * ff_half, ff_half)], hid, load_sem.at[1]
    )
    load_slots_a = pltpu.make_async_copy(slots_a_hbm, slots_a, load_sem.at[4])
    load_slots_b = pltpu.make_async_copy(slots_b_hbm, slots_b, load_sem.at[5])
    load_slots_b.start()
    load_slots_a.start()
    load_grad.start()

    def load_weight(c):
        place = pl.ds(pl.multiple_of(c * TILE, TILE), TILE)
        return pltpu.make_async_copy(weight_hbm.at[place, :], weight.at[place, :], weight_sem.at[c])

    def start_weight(c, _):
        load_weight(c).start()
        return 0

    load_weight(0).start()
    load_weight(1).start()

    at_all = at_own * n_pair + at_t
    n_all = n_own * n_pair
    barrier = pltpu.get_barrier_semaphore()

    def greet(k, _):
        i = lax.rem(at_all + k, n_all)
        pl.semaphore_signal(
            barrier,
            inc=1,
            device_id=dev(
                lax.div(i, n_data * n_pair), lax.rem(lax.div(i, n_pair), n_data), lax.rem(i, n_pair)
            ),
            device_id_type=MESH,
        )
        return 0

    lax.fori_loop(1, n_all, greet, 0)

    n_slot = slots_a.shape[0]
    seg = tok // seg_ref.shape[0]

    def slots_of(d):
        ids = ids_ref[d]
        slots = jnp.zeros_like(ids)
        for i in range(table_ref.shape[0]):
            slots = jnp.where(ids == i, table_ref[i], slots)
        return slots

    pick = [
        [
            jnp.max(
                jnp.where(slots_of(d) == at_own * n_slot + l, 1.0, 0.0), axis=1, keepdims=True
            )
            for l in range(n_slot)
        ]
        for d in range(n_data)
    ]
    spot = lax.broadcasted_iota(jnp.int32, (1, tok), 1)
    limit = jnp.zeros((1, tok), jnp.int32)
    for i in range(tok // seg):
        limit = jnp.where(spot >= i * seg, seg_ref[i] + i * seg, limit)
    my_owner = lax.shift_right_logical(slots_of(at_d), 1)
    my_owner = jnp.where(spot < limit, my_owner, n_own)
    owner_ids = lax.broadcasted_iota(jnp.int32, (n_own, tok), 0)
    choose_ref[...] = jnp.where(owner_ids == my_owner, 1.0, 0.0)
    data_ids = lax.broadcasted_iota(jnp.int32, (n_data, tok), 0)
    choose_mine_ref[...] = jnp.where(data_ids + at_a * n_data == my_owner, 1.0, 0.0)
    row_in_seg = lax.broadcasted_iota(jnp.int32, (seg, 128), 0)
    for i in range(half // seg):
        live = seg_ref[at_t * (half // seg) + i]
        live_ref[i * seg : (i + 1) * seg, :] = jnp.where(row_in_seg < live, 1.0, 0.0)

    def choose_slots(slots, sent, size):
        def step(i, _):
            place = lanes(i * size, size)
            for d in range(n_data):
                total = slots[0, :, place].astype(jnp.float32) * pick[d][0]
                for l in range(1, n_slot):
                    total += slots[l, :, place].astype(jnp.float32) * pick[d][l]
                sent[d, :, place] = total.astype(jnp.bfloat16)
            return 0

        lax.fori_loop(0, slots.shape[2] // size, step, 0)

    load_slots_b.wait()
    choose_slots(slots_b, sent_b, 512)
    pl.semaphore_wait(barrier, n_all - 1)

    b_copies = [
        pltpu.make_async_copy(
            sent_b.at[at_d], panels_b.at[rows(at_d * rank, rank), :], load_sem.at[2]
        )
    ]
    for k in range(1, n_data):
        j = lax.rem(at_d + k, n_data)
        b_copies.append(
            remote(
                sent_b.at[j],
                panels_b.at[rows(at_d * rank, rank), :],
                b_send.at[k],
                b_recv.at[k],
                dev(at_a, j, at_t),
            )
        )
    for copy in b_copies:
        copy.start()

    load_slots_a.wait()
    choose_slots(slots_a, sent_a, 512)

    mine = lanes(at_t * ff_half, ff_half)
    a_copies = [
        pltpu.make_async_copy(
            sent_a.at[at_d, :, lanes(at_a * ff + at_t * ff_half, ff_half)],
            panels_a.at[rows(at_own * rank, rank), mine],
            load_sem.at[3],
        )
    ]
    for k in range(1, n_own):
        o = lax.rem(at_own + k, n_own)
        a2, d2 = lax.div(o, n_data), lax.rem(o, n_data)
        a_copies.append(
            remote(
                sent_a.at[d2, :, lanes(a2 * ff + at_t * ff_half, ff_half)],
                panels_a.at[rows(at_own * rank, rank), mine],
                a_send.at[k],
                a_recv.at[k],
                dev(a2, d2, at_t),
            )
        )
    for copy in a_copies:
        copy.start()
    lax.fori_loop(2, 6, start_weight, 0)
    load_hid.start()
    lax.fori_loop(6, n_tile, start_weight, 0)
    load_grad.wait()

    pair_dev = dev(at_a, at_d, 1 - at_t)

    def pair_copy(c):
        return remote(to_pair.at[c], from_pair.at[c], pair_send.at[c], pair_recv.at[c], pair_dev)

    forward = remote(
        panels_a.at[:, mine], panels_a.at[:, mine], fwd_sem.at[0], fwd_sem.at[1], pair_dev
    )

    def sum_peer(k):
        q = lax.rem(at_sum + k, n_sum)
        return q, dev(lax.div(q, n_pair), at_d, lax.rem(q, n_pair))

    def scatter_copies(w):
        copies = []
        for k in range(1, n_sum):
            q, to = sum_peer(k)
            copies.append(
                remote(
                    part.at[w, q], part_in.at[w, k], rs_send.at[w, k], rs_recv.at[w, k], to
                )
            )
        return copies

    def gather_copies(w):
        copies = []
        for k in range(1, n_sum):
            _, to = sum_peer(k)
            copies.append(
                remote(
                    low.at[w, at_sum], low.at[w, at_sum], ag_send.at[w, k], ag_recv.at[w, k], to
                )
            )
        return copies

    def start_all(copies):
        for copy in copies:
            copy.start()

    def wait_all(copies):
        for copy in copies:
            copy.wait()

    def store_part(w, i, value):
        for s in range(TILE // tok_piece):
            part[w, i * (TILE // tok_piece) + s] = value[:, s * tok_piece : (s + 1) * tok_piece]

    def part_v():
        wait_all(b_copies)

        def step(i, _):
            block = grad[pl.ds(pl.multiple_of(i * TILE, TILE), TILE), :]
            wide = lax.dot_general(panels_b[...], block, NT, preferred_element_type=jnp.float32)
            total = jnp.zeros((rank, TILE), jnp.float32)
            for j in range(n_data):
                keep = choose_mine_ref[j : j + 1, lanes(i * TILE, TILE)]
                total += wide[j * rank : (j + 1) * rank] * keep
            store_part(1, i, total)
            return 0

        lax.fori_loop(0, tok // TILE, step, 0)
        start_all(scatter_copies(1))

    def part_u():
        wait_all(a_copies)
        forward.start()

        def step(i, _):
            block = hid[pl.ds(pl.multiple_of(i * TILE, TILE), TILE), :]
            wide = lax.dot_general(
                panels_a[:, mine], block, NT, preferred_element_type=jnp.float32
            )
            total = jnp.zeros((rank, TILE), jnp.float32)
            for o in range(n_own):
                keep = choose_ref[o : o + 1, lanes(i * TILE, TILE)]
                total += wide[o * rank : (o + 1) * rank] * keep
            store_part(0, i, total)
            return 0

        lax.fori_loop(0, tok // TILE, step, 0)
        start_all(scatter_copies(0))

    def sum_low(w):
        wait_all(scatter_copies(w))
        total = part[w, at_sum]
        for k in range(1, n_sum):
            total += part_in[w, k]
        low[w, at_sum] = total.astype(jnp.bfloat16)
        start_all(gather_copies(w))

    def use_v():
        wait_all(gather_copies(1))
        for i in range(n_sum):
            value = low[1, i].astype(jnp.float32) * adapter_scale
            place = slice(i * tok_piece, (i + 1) * tok_piece)
            for o in range(n_own):
                spread[o * rank : (o + 1) * rank, place] = (
                    value * choose_ref[o : o + 1, place]
                ).astype(jnp.bfloat16)
        load_hid.wait()

        def step(i, _):
            place = lanes(i * TILE, TILE)
            piece_a[:, place] = jnp.dot(
                spread[...], hid[:, place], preferred_element_type=jnp.float32
            ).astype(jnp.bfloat16)
            return 0

        lax.fori_loop(0, ff_half // TILE, step, 0)
        spread_own[...] = jnp.transpose(
            spread[:, lanes(at_t * half, half)].astype(jnp.float32)
        ).astype(jnp.bfloat16)
        return_a(True)

    ratio = n_adapter // n_pair
    core = lax.div(at_a, ratio)
    low_a = lax.rem(at_a, ratio)
    ret_slot = (low_a * n_data + at_d) * n_pair + at_t
    ret_place = lanes(low_a * ff + at_t * ff_half, ff_half)

    def return_copy(k):
        o = lax.rem(at_own + k, n_own)
        return remote(
            piece_a.at[rows(o * rank, rank), :],
            back_a.at[at_d, :, ret_place],
            ra_send.at[k],
            ra_recv.at[ret_slot],
            dev(lax.div(o, n_data), lax.rem(o, n_data), core),
        )

    def return_a(start):
        for k in range(1, n_own):
            if start:
                return_copy(k).start()
            else:
                return_copy(k).wait_send()

        @pl.when(at_t != core)
        def _():
            if start:
                return_copy(0).start()
            else:
                return_copy(0).wait_send()

        if start:

            @pl.when(at_t == core)
            def _():
                pltpu.make_async_copy(
                    piece_a.at[rows(at_own * rank, rank), :],
                    back_a.at[at_d, :, ret_place],
                    ra_recv.at[ret_slot],
                ).start()

    def wait_returned():
        for s in range(ratio * n_data * n_pair):
            a2, d2, t2 = s // (n_data * n_pair), s // n_pair % n_data, s % n_pair
            first = a2 * ff + t2 * ff_half
            place = back_a.at[d2, :, first : first + ff_half]
            remote(place, place, ra_send.at[0], ra_recv.at[s], pair_dev).wait_recv()

    def return_b():
        copies = []
        for k in range(1, n_data):
            j = lax.rem(at_d + k, n_data)
            copies.append(
                remote(
                    piece_b.at[j], back_b.at[at_d], rb_send.at[k], rb_recv.at[k], dev(at_a, j, at_t)
                )
            )
        return copies

    def use_u():
        wait_all(gather_copies(0))
        parts = []
        for i in range(n_sum):
            value = low[0, i].astype(jnp.float32) * adapter_scale
            place = slice(i * tok_piece, (i + 1) * tok_piece)
            parts.append(
                jnp.concatenate(
                    [
                        value * choose_mine_ref[j : j + 1, place]
                        for j in range(n_data)
                    ],
                    axis=0,
                ).astype(jnp.bfloat16)
            )
        spread_u = jnp.concatenate(parts, axis=1)
        back_b[at_d] = jnp.zeros_like(back_b[0])
        for i in range(width // 512):
            place = slice(i * 512, (i + 1) * 512)
            wide = jnp.dot(spread_u, grad[:, place], preferred_element_type=jnp.float32)
            for j in range(n_data):
                piece_b[j, :, place] = wide[j * rank : (j + 1) * rank]
        start_all(return_b())

    events = {
        1: part_v,
        3: lambda: sum_low(1),
        5: use_v,
        7: part_u,
        9: lambda: sum_low(0),
        11: use_u,
    }

    def main(c, _):
        load_weight(c).wait()
        w = weight[pl.ds(pl.multiple_of(c * TILE, TILE), TILE), :]
        both = lax.dot_general(grad[...], w, NT, preferred_element_type=jnp.float32)
        to_pair[c] = jnp.where(at_t == 0, both[half:], both[:half]).astype(jnp.bfloat16)
        own_acc[c] = jnp.where(at_t == 0, both[:half], both[half:])
        pair_copy(c).start()
        for at, event in events.items():
            pl.when(c == min(at, n_tile - 1))(event)
        return 0

    lax.fori_loop(0, n_tile, main, 0)
    forward.wait()

    def store_copy(c):
        return pltpu.make_async_copy(staged.at[c], out_hbm.at[:, lanes(c * TILE, TILE)], out_sem.at[c])

    def finish(c, _):
        pair_copy(c).wait()
        total = own_acc[c] + from_pair[c].astype(jnp.float32)
        total += jnp.dot(
            spread_own[...], panels_a[:, lanes(c * TILE, TILE)], preferred_element_type=jnp.float32
        )
        for i in range(TILE // 128):
            place = slice(i * 128, (i + 1) * 128)
            staged[c, :, place] = jnp.where(live_ref[...] > 0, total[:, place], 0.0).astype(
                jnp.bfloat16
            )
        store_copy(c).start()
        return 0

    lax.fori_loop(0, n_tile, finish, 0)

    wait_all(return_b())
    for l in range(n_slot):
        total = jnp.zeros_like(piece_b[0])
        for d in range(n_data):
            from_here = jnp.where(at_d == d, 1.0, 0.0) * pick[d][l]
            total += piece_b[d] * from_here
            total += back_b[d] * (pick[d][l] - from_here)
        grad_b_ref[l] = total
    return_a(False)
    wait_returned()
    for l in range(n_slot):
        total = back_a[0].astype(jnp.float32) * pick[0][l]
        for d in range(1, n_data):
            total += back_a[d].astype(jnp.float32) * pick[d][l]
        grad_a_ref[l] = total

    def drain(c, _):
        store_copy(c).wait()
        return 0

    lax.fori_loop(0, n_tile, drain, 0)


def fused_on_device(
    output_gradient,
    hidden,
    frozen_down_weight,
    adapter_input_panels,
    adapter_output_panels,
    token_adapter_table,
    adapter_slot_table,
    segment_live_tokens,
):
    tok, width = output_gradient.shape
    ff = hidden.shape[1]
    n_slot, rank, ff_all = adapter_input_panels.shape
    n_adapter = lax.axis_size("adapter")
    n_data = lax.axis_size("dp")
    n_pair = lax.axis_size("tensor")
    n_own = n_adapter * n_data
    n_sum = n_adapter * n_pair
    half = tok // n_pair
    ff_half = ff // n_pair
    n_tile = ff // TILE
    anywhere = pl.BlockSpec(memory_space=pl.ANY)
    vmem = pl.BlockSpec(memory_space=pltpu.VMEM)
    smem = pl.BlockSpec(memory_space=pltpu.SMEM)
    dma = pltpu.SemaphoreType.DMA
    bf16, f32 = jnp.bfloat16, jnp.float32
    ff_out = ff_all // n_pair
    n_back = n_adapter // n_pair * n_data * n_pair
    outs = pl.pallas_call(
        functools.partial(fused_kernel, (n_adapter, n_data, n_pair, rank)),
        out_shape=(
            jax.ShapeDtypeStruct((half, ff), bf16),
            jax.ShapeDtypeStruct((n_slot, rank, ff_out), f32),
            jax.ShapeDtypeStruct((n_slot, rank, width), f32),
        ),
        in_specs=[anywhere] * 5 + [vmem, smem, smem],
        out_specs=(anywhere, vmem, vmem),
        scratch_shapes=[
            pltpu.VMEM((tok, width), bf16),
            pltpu.VMEM((tok, ff_half), bf16),
            pltpu.VMEM((ff, width), bf16),
            pltpu.VMEM((n_slot, rank, ff_all), bf16),
            pltpu.VMEM((n_slot, rank, width), bf16),
            pltpu.VMEM((n_data, rank, ff_all), bf16),
            pltpu.VMEM((n_data, rank, width), bf16),
            pltpu.VMEM((n_own, tok), f32),
            pltpu.VMEM((n_data, tok), f32),
            pltpu.VMEM((half, 128), f32),
            pltpu.VMEM((n_own * rank, ff), bf16),
            pltpu.VMEM((n_data * rank, width), bf16),
            pltpu.VMEM((n_tile, half, TILE), f32),
            pltpu.VMEM((n_tile, half, TILE), bf16),
            pltpu.VMEM((n_tile, half, TILE), bf16),
            pltpu.VMEM((n_tile, half, TILE), bf16),
            pltpu.VMEM((2, n_sum, rank, tok // n_sum), f32),
            pltpu.VMEM((2, n_sum, rank, tok // n_sum), f32),
            pltpu.VMEM((2, n_sum, rank, tok // n_sum), bf16),
            pltpu.VMEM((n_own * rank, tok), bf16),
            pltpu.VMEM((half, n_own * rank), bf16),
            pltpu.VMEM((n_own * rank, ff_half), bf16),
            pltpu.VMEM((n_data, rank, ff_out), bf16),
            pltpu.VMEM((n_data, rank, width), f32),
            pltpu.VMEM((n_data, rank, width), f32),
            dma((6,)),
            dma((n_tile,)),
            dma((n_tile,)),
            dma((n_own,)),
            dma((n_own,)),
            dma((n_data,)),
            dma((n_data,)),
            dma((n_tile,)),
            dma((n_tile,)),
            dma((2,)),
            dma((2, n_sum)),
            dma((2, n_sum)),
            dma((2, n_sum)),
            dma((2, n_sum)),
            dma((n_own,)),
            dma((n_back,)),
            dma((n_data,)),
            dma((n_data,)),
        ],
        compiler_params=pltpu.CompilerParams(
            collective_id=0, has_side_effects=True, vmem_limit_bytes=60 * 1024 * 1024
        ),
        cost_estimate=pl.CostEstimate(
            flops=2 * tok * width * ff, bytes_accessed=2 * ff * width, transcendentals=0
        ),
    )(
        output_gradient,
        hidden,
        frozen_down_weight,
        adapter_input_panels,
        adapter_output_panels,
        token_adapter_table.reshape(n_data, 1, tok),
        adapter_slot_table,
        segment_live_tokens,
    )
    return tuple(copy_out(outs))


def copy_kernel(n_arrays, n_cuts, *refs):
    copies = []
    sems = refs[2 * n_arrays]
    for a in range(n_arrays):
        src, dst = refs[a], refs[n_arrays + a]
        rows = src.shape[0] // n_cuts[a]
        for i in range(n_cuts[a]):
            place = slice(i * rows, (i + 1) * rows)
            copies.append(
                pltpu.make_async_copy(src.at[place], dst.at[place], sems.at[len(copies)])
            )
    for copy in copies:
        copy.start()
    for copy in copies:
        copy.wait()


def copy_out(arrays):
    anywhere = pl.BlockSpec(memory_space=pl.ANY)
    cuts = [8 if array.ndim == 2 else array.shape[0] for array in arrays]
    size = sum(array.size * array.dtype.itemsize for array in arrays)
    return pl.pallas_call(
        functools.partial(copy_kernel, len(arrays), cuts),
        out_shape=[jax.ShapeDtypeStruct(array.shape, array.dtype) for array in arrays],
        in_specs=[anywhere] * len(arrays),
        out_specs=[anywhere] * len(arrays),
        scratch_shapes=[pltpu.SemaphoreType.DMA((sum(cuts),))],
        cost_estimate=pl.CostEstimate(flops=0, bytes_accessed=2 * size, transcendentals=0),
    )(*arrays)


def fits_kernel(hidden, adapter_input_panels):
    ff = hidden.shape[1]
    n_slot, rank, _ = adapter_input_panels.shape
    n_adapter = lax.axis_size("adapter")
    n_data = lax.axis_size("dp")
    n_pair = lax.axis_size("tensor")
    n_sum = n_adapter * n_pair
    return (
        n_pair == 2
        and n_slot == 2
        and rank == 16
        and n_adapter % n_pair == 0
        and ff % (n_pair * TILE) == 0
        and ff // TILE > 11
        and hidden.shape[0] == n_sum * 128
        and n_adapter * n_data * rank <= 256
        and adapter_input_panels.shape[2] % 512 == 0
    )


def on_device(*args):
    if fits_kernel(args[1], args[3]):
        return fused_on_device(*args)
    return plain_on_device(*args)


def solution(mesh):
    placed = (
        P(("groups", "dp"), "tensor"),
        P(("groups", "dp"), "adapter"),
        P("adapter", "tensor"),
        P(("groups", "adapter", "dp"), None, None),
        P(("groups", "adapter", "dp"), None, "tensor"),
        P("groups"),
        P("groups"),
        P(("groups", "dp")),
    )
    return jax.shard_map(
        on_device,
        mesh=mesh,
        in_specs=placed,
        out_specs=(
            P(("groups", "dp", "tensor"), "adapter"),
            P(("groups", "adapter", "dp"), None, "tensor"),
            P(("groups", "adapter", "dp"), None, "tensor"),
        ),
        check_vma=False,
    )
```

```python
import functools

import jax
import jax.numpy as jnp
from jax import lax
from jax.experimental import pallas as pl
from jax.experimental.pallas import tpu as pltpu
from jax.sharding import PartitionSpec as P

adapter_scale = 4.0
MESH = pl.DeviceIdType.MESH
NT = (((1,), (1,)), ((), ()))
TILE = 256


def lookup(keys_row, table):
    positions = jnp.arange(table.shape[0], dtype=jnp.int32)
    picked = jnp.where(keys_row[:, None] == positions[None, :], table[None, :], 0)
    return jnp.sum(picked, axis=1)


def plain_on_device(
    output_gradient,
    hidden,
    frozen_down_weight,
    adapter_input_panels,
    adapter_output_panels,
    token_adapter_table,
    adapter_slot_table,
    segment_live_tokens,
):
    tok_rows = output_gradient.shape[0]
    half_width = output_gradient.shape[1]
    ff_share = hidden.shape[1]
    owned_slot_list = adapter_input_panels.shape[0]
    rank_extent = adapter_input_panels.shape[1]
    n_adapter = lax.axis_size("adapter")
    n_data = lax.axis_size("dp")
    n_pair = lax.axis_size("tensor")
    capacity = owned_slot_list // 2
    owners = n_adapter * n_data
    n_slots = owners * owned_slot_list
    d_piece = half_width // n_adapter
    ff_piece = ff_share // n_pair
    half_rows = tok_rows // n_pair
    n_recv = owners * capacity
    segment_rows = tok_rows // segment_live_tokens.shape[0]
    at_adapter = lax.axis_index("adapter")
    at_data = lax.axis_index("dp")
    at_pair = lax.axis_index("tensor")
    at_owner = at_adapter * n_data + at_data
    slot_ids = jnp.arange(n_slots, dtype=jnp.int32)
    token_slot = lookup(token_adapter_table, adapter_slot_table).reshape(n_data, tok_rows)
    used_flags = jnp.any(token_slot[:, :, None] == slot_ids[None, None, :], axis=1).astype(
        jnp.int32
    )
    used_blocks = used_flags.reshape(n_data, owners, owned_slot_list)
    order_in_block = jnp.cumsum(used_blocks, axis=2) - 1
    mine_used = lax.dynamic_index_in_dim(used_blocks, at_owner, 1, False)
    mine_order = lax.dynamic_index_in_dim(order_in_block, at_owner, 1, False)
    cap_ids = jnp.arange(capacity, dtype=jnp.int32)
    picks = (mine_used[:, None, :] == 1) & (mine_order[:, None, :] == cap_ids[None, :, None])
    lower_selection = picks.astype(jnp.bfloat16)
    picks_full = picks.astype(jnp.float32)
    sent_a = jnp.einsum(
        "mjt,tou->mjou", lower_selection, adapter_input_panels, preferred_element_type=jnp.float32
    ).astype(jnp.bfloat16)
    sent_b = jnp.einsum(
        "tke,eop->tkop", lower_selection, adapter_output_panels, preferred_element_type=jnp.float32
    ).astype(jnp.bfloat16)
    sent_a = sent_a.reshape(n_data, capacity, rank_extent, n_adapter, ff_share).transpose(
        3, 0, 1, 2, 4
    )
    sent_b = sent_b.reshape(n_data, capacity, rank_extent, n_adapter, d_piece).transpose(
        3, 0, 1, 2, 4
    )
    flat_a = sent_a.reshape(n_recv, rank_extent, ff_share)
    flat_b = sent_b.reshape(n_recv, rank_extent, d_piece)
    got_a, got_b = (
        lax.all_to_all(flat_a, ("adapter", "dp"), split_axis=0, concat_axis=0, tiled=True),
        lax.all_to_all(flat_b, ("adapter", "dp"), split_axis=0, concat_axis=0, tiled=True),
    )
    panels_a = got_a.reshape(n_recv * rank_extent, ff_share)
    panels_b = got_b.reshape(n_recv * rank_extent, d_piece)
    my_slots = lax.dynamic_index_in_dim(token_slot, at_data, 0, False)
    my_order = lax.dynamic_index_in_dim(order_in_block, at_data, 0, False).reshape(n_slots)
    recv_index = my_slots // owned_slot_list * capacity + lookup(my_slots, my_order)
    recv_ids = jnp.arange(n_recv, dtype=jnp.int32)
    select = (recv_index[:, None] == recv_ids[None, :])[:, :, None]
    seg_pos = jnp.arange(segment_rows, dtype=jnp.int32)
    live_mask = (seg_pos[None, :] < segment_live_tokens[:, None]).reshape(tok_rows)
    live_grad = jnp.where(live_mask[:, None], output_gradient, jnp.zeros_like(output_gradient))
    hidden_part = lax.dynamic_slice_in_dim(hidden, at_pair * ff_piece, ff_piece, 1)
    panels_part = lax.dynamic_slice_in_dim(panels_a, at_pair * ff_piece, ff_piece, 1)
    grad_piece = lax.dynamic_slice_in_dim(live_grad, at_adapter * d_piece, d_piece, 1)
    wide_u = jnp.einsum("tf,kf->tk", hidden_part, panels_part, preferred_element_type=jnp.float32)
    wide_v = jnp.einsum("td,kd->tk", grad_piece, panels_b, preferred_element_type=jnp.float32)
    part_u = jnp.sum(jnp.where(select, wide_u.reshape(tok_rows, n_recv, rank_extent), 0.0), axis=1)
    part_v = jnp.sum(jnp.where(select, wide_v.reshape(tok_rows, n_recv, rank_extent), 0.0), axis=1)
    full_u, full_v = lax.psum((part_u, part_v), ("adapter", "tensor"))
    first_round_result = full_u.astype(jnp.bfloat16)
    second_round_result = full_v.astype(jnp.bfloat16)
    zero_low = jnp.zeros((), jnp.bfloat16)
    spread_u = jnp.where(select, first_round_result[:, None, :], zero_low).reshape(
        tok_rows, n_recv * rank_extent
    )
    spread_v = jnp.where(select, second_round_result[:, None, :], zero_low).reshape(
        tok_rows, n_recv * rank_extent
    )
    frozen_portion = lax.psum_scatter(
        jnp.einsum("td,fd->tf", live_grad, frozen_down_weight, preferred_element_type=jnp.float32),
        "tensor",
        scatter_dimension=0,
        tiled=True,
    )
    spread_half = lax.dynamic_slice_in_dim(spread_v, at_pair * half_rows, half_rows, 0)
    hidden_half = lax.dynamic_slice_in_dim(hidden, at_pair * half_rows, half_rows, 0)
    adapter_token_rows = jnp.dot(spread_half, panels_a, preferred_element_type=jnp.float32)
    hidden_gradient = (frozen_portion + adapter_scale * adapter_token_rows).astype(jnp.bfloat16)
    input_portion = adapter_scale * jnp.einsum(
        "tk,tf->kf", spread_half, hidden_half, preferred_element_type=jnp.float32
    )
    output_portion = adapter_scale * jnp.einsum(
        "tk,td->kd", spread_u, grad_piece, preferred_element_type=jnp.float32
    )
    a_width = input_portion.shape[1]
    back_a = input_portion.reshape(n_adapter, n_data, capacity, rank_extent, a_width)
    back_b = output_portion.reshape(n_adapter, n_data, capacity, rank_extent, d_piece)
    flat_back_a = back_a.reshape(n_recv, rank_extent, a_width)
    flat_back_b = back_b.reshape(n_recv, rank_extent, d_piece)
    ret_a, ret_b = (
        lax.all_to_all(flat_back_a, ("adapter", "dp"), split_axis=0, concat_axis=0, tiled=True),
        lax.all_to_all(flat_back_b, ("adapter", "dp"), split_axis=0, concat_axis=0, tiled=True),
    )
    ret_a = ret_a.reshape(n_adapter, n_data, capacity, rank_extent, a_width)
    ret_b = ret_b.reshape(n_adapter, n_data, capacity, rank_extent, d_piece)
    own_a = jnp.einsum("jcl,kjcrf->lrkf", picks_full, ret_a, precision=lax.Precision.HIGHEST)
    own_b = jnp.einsum("jcl,kjcrd->lrkd", picks_full, ret_b, precision=lax.Precision.HIGHEST)
    own_b = own_b.reshape(owned_slot_list, rank_extent, half_width)
    own_a = own_a.reshape(owned_slot_list, rank_extent, n_adapter * a_width)
    grad_a = lax.psum_scatter(own_a, "tensor", scatter_dimension=2, tiled=True)
    return (hidden_gradient, grad_a, own_b)


def fused_kernel(
    sizes,
    grad_hbm,
    hidden_hbm,
    weight_hbm,
    slots_a_hbm,
    slots_b_hbm,
    ids_ref,
    table_ref,
    seg_ref,
    out_hbm,
    grad_a_ref,
    grad_b_ref,
    grad,
    hid,
    weight,
    slots_a,
    slots_b,
    sent_a,
    sent_b,
    choose_ref,
    choose_mine_ref,
    live_ref,
    panels_a,
    panels_b,
    own_acc,
    to_pair,
    from_pair,
    staged,
    part,
    part_in,
    low,
    spread,
    spread_own,
    piece_a,
    back_a,
    piece_b,
    back_b,
    load_sem,
    weight_sem,
    out_sem,
    a_send,
    a_recv,
    b_send,
    b_recv,
    pair_send,
    pair_recv,
    fwd_sem,
    rs_send,
    rs_recv,
    ag_send,
    ag_recv,
    ra_send,
    ra_recv,
    rb_send,
    rb_recv,
):
    n_adapter, n_data, n_pair, rank = sizes
    tok, width = grad.shape
    half = tok // n_pair
    ff_half = hid.shape[1]
    ff = ff_half * n_pair
    n_own = n_adapter * n_data
    n_sum = n_adapter * n_pair
    tok_piece = tok // n_sum
    n_tile = ff // TILE
    at_g = lax.axis_index("groups")
    at_a = lax.axis_index("adapter")
    at_d = lax.axis_index("dp")
    at_t = lax.axis_index("tensor")
    at_own = at_a * n_data + at_d
    at_sum = at_a * n_pair + at_t

    def dev(a, d, t):
        return (at_g, a, d, t)

    far_first = sorted(range(1, n_own), key=lambda k: -min(k, n_own - k))

    def remote(src, dst, send, recv, to):
        return pltpu.make_async_remote_copy(
            src_ref=src, dst_ref=dst, send_sem=send, recv_sem=recv, device_id=to, device_id_type=MESH
        )

    def lanes(start, size):
        return pl.ds(pl.multiple_of(start, 128), size)

    def rows(start, size):
        return pl.ds(pl.multiple_of(start, 16), size)

    load_grad = pltpu.make_async_copy(grad_hbm, grad, load_sem.at[0])
    load_hid = pltpu.make_async_copy(
        hidden_hbm.at[:, lanes(at_t * ff_half, ff_half)], hid, load_sem.at[1]
    )
    load_slots_a = pltpu.make_async_copy(slots_a_hbm, slots_a, load_sem.at[4])
    load_slots_b = pltpu.make_async_copy(slots_b_hbm, slots_b, load_sem.at[5])
    load_slots_b.start()
    load_slots_a.start()
    load_grad.start()

    def load_weight(c):
        place = pl.ds(pl.multiple_of(c * TILE, TILE), TILE)
        return pltpu.make_async_copy(weight_hbm.at[place, :], weight.at[place, :], weight_sem.at[c])

    def start_weight(c, _):
        load_weight(c).start()
        return 0

    load_weight(0).start()
    load_weight(1).start()

    at_all = at_own * n_pair + at_t
    n_all = n_own * n_pair
    barrier = pltpu.get_barrier_semaphore()

    def greet(k, _):
        i = lax.rem(at_all + k, n_all)
        pl.semaphore_signal(
            barrier,
            inc=1,
            device_id=dev(
                lax.div(i, n_data * n_pair), lax.rem(lax.div(i, n_pair), n_data), lax.rem(i, n_pair)
            ),
            device_id_type=MESH,
        )
        return 0

    lax.fori_loop(1, n_all, greet, 0)

    n_slot = slots_a.shape[0]
    seg = tok // seg_ref.shape[0]

    def slots_of(d):
        ids = ids_ref[d]
        slots = jnp.zeros_like(ids)
        for i in range(table_ref.shape[0]):
            slots = jnp.where(ids == i, table_ref[i], slots)
        return slots

    pick = [
        [
            jnp.max(
                jnp.where(slots_of(d) == at_own * n_slot + l, 1.0, 0.0), axis=1, keepdims=True
            )
            for l in range(n_slot)
        ]
        for d in range(n_data)
    ]
    def choose_slots(slots, sent, size):
        def step(i, _):
            place = lanes(i * size, size)
            for d in range(n_data):
                total = slots[0, :, place].astype(jnp.float32) * pick[d][0]
                for l in range(1, n_slot):
                    total += slots[l, :, place].astype(jnp.float32) * pick[d][l]
                sent[d, :, place] = total.astype(jnp.bfloat16)
            return 0

        lax.fori_loop(0, slots.shape[2] // size, step, 0)

    pl.semaphore_wait(barrier, n_all - 1)
    load_slots_b.wait()
    choose_slots(slots_b, sent_b, 512)
    b_copies = [
        pltpu.make_async_copy(
            sent_b.at[at_d], panels_b.at[rows(at_d * rank, rank), :], load_sem.at[2]
        )
    ]
    for k in range(1, n_data):
        j = lax.rem(at_d + k, n_data)
        b_copies.append(
            remote(
                sent_b.at[j],
                panels_b.at[rows(at_d * rank, rank), :],
                b_send.at[k],
                b_recv.at[k],
                dev(at_a, j, at_t),
            )
        )
    for copy in b_copies:
        copy.start()

    load_slots_a.wait()
    choose_slots(slots_a, sent_a, ff_half)

    mine = lanes(at_t * ff_half, ff_half)
    a_copies = [
        pltpu.make_async_copy(
            sent_a.at[at_d, :, lanes(at_a * ff + at_t * ff_half, ff_half)],
            panels_a.at[rows(at_own * rank, rank), mine],
            load_sem.at[3],
        )
    ]
    for k in far_first:
        o = lax.rem(at_own + k, n_own)
        a2, d2 = lax.div(o, n_data), lax.rem(o, n_data)
        a_copies.append(
            remote(
                sent_a.at[d2, :, lanes(a2 * ff + at_t * ff_half, ff_half)],
                panels_a.at[rows(at_own * rank, rank), mine],
                a_send.at[k],
                a_recv.at[k],
                dev(a2, d2, at_t),
            )
        )
    for copy in a_copies:
        copy.start()
    lax.fori_loop(2, 6, start_weight, 0)
    load_hid.start()
    lax.fori_loop(6, n_tile, start_weight, 0)
    load_grad.wait()

    spot = lax.broadcasted_iota(jnp.int32, (1, tok), 1)
    limit = jnp.zeros((1, tok), jnp.int32)
    for i in range(tok // seg):
        limit = jnp.where(spot >= i * seg, seg_ref[i] + i * seg, limit)
    my_owner = lax.shift_right_logical(slots_of(at_d), 1)
    my_owner = jnp.where(spot < limit, my_owner, n_own)
    owner_ids = lax.broadcasted_iota(jnp.int32, (n_own, tok), 0)
    choose_ref[...] = jnp.where(owner_ids == my_owner, 1.0, 0.0)
    data_ids = lax.broadcasted_iota(jnp.int32, (n_data, tok), 0)
    choose_mine_ref[...] = jnp.where(data_ids + at_a * n_data == my_owner, 1.0, 0.0)
    row_in_seg = lax.broadcasted_iota(jnp.int32, (seg, 128), 0)
    for i in range(half // seg):
        live = seg_ref[at_t * (half // seg) + i]
        live_ref[i * seg : (i + 1) * seg, :] = jnp.where(row_in_seg < live, 1.0, 0.0)


    pair_dev = dev(at_a, at_d, 1 - at_t)

    def pair_copy(c):
        return remote(to_pair.at[c], from_pair.at[c], pair_send.at[c], pair_recv.at[c], pair_dev)

    forward = remote(
        panels_a.at[:, mine], panels_a.at[:, mine], fwd_sem.at[0], fwd_sem.at[1], pair_dev
    )

    def sum_peer(k):
        q = lax.rem(at_sum + k, n_sum)
        return q, dev(lax.div(q, n_pair), at_d, lax.rem(q, n_pair))

    def scatter_copies():
        copies = []
        for k in range(1, n_sum):
            q, to = sum_peer(k)
            copies.append(
                remote(
                    part.at[q], part_in.at[k], rs_send.at[k], rs_recv.at[k], to
                )
            )
        return copies

    def gather_copies():
        copies = []
        for k in range(1, n_sum):
            _, to = sum_peer(k)
            copies.append(
                remote(
                    low.at[at_sum], low.at[at_sum], ag_send.at[k], ag_recv.at[k], to
                )
            )
        return copies

    def start_all(copies):
        for copy in copies:
            copy.start()

    def wait_all(copies):
        for copy in copies:
            copy.wait()

    def store_part(w, i, value):
        for s in range(TILE // tok_piece):
            part[i * (TILE // tok_piece) + s, w] = value[:, s * tok_piece : (s + 1) * tok_piece]

    def part_v():
        wait_all(b_copies)

        def step(i, _):
            block = grad[pl.ds(pl.multiple_of(i * TILE, TILE), TILE), :]
            wide = lax.dot_general(panels_b[...], block, NT, preferred_element_type=jnp.float32)
            total = jnp.zeros((rank, TILE), jnp.float32)
            for j in range(n_data):
                keep = choose_mine_ref[j : j + 1, lanes(i * TILE, TILE)]
                total += wide[j * rank : (j + 1) * rank] * keep
            store_part(1, i, total)
            return 0

        lax.fori_loop(0, tok // TILE, step, 0)

    def part_u():
        wait_all(a_copies)
        load_hid.wait()
        forward.start()

        def step(i, _):
            block = hid[pl.ds(pl.multiple_of(i * TILE, TILE), TILE), :]
            wide = lax.dot_general(
                panels_a[:, mine], block, NT, preferred_element_type=jnp.float32
            )
            total = jnp.zeros((rank, TILE), jnp.float32)
            for o in range(n_own):
                keep = choose_ref[o : o + 1, lanes(i * TILE, TILE)]
                total += wide[o * rank : (o + 1) * rank] * keep
            store_part(0, i, total)
            return 0

        lax.fori_loop(0, tok // TILE, step, 0)
        start_all(scatter_copies())

    def sum_low():
        wait_all(scatter_copies())
        total = part[at_sum]
        for k in range(1, n_sum):
            total += part_in[k]
        low[at_sum] = total.astype(jnp.bfloat16)
        start_all(gather_copies())

    def use_v():
        wait_all(gather_copies())
        for i in range(n_sum):
            value = low[i, 1].astype(jnp.float32) * adapter_scale
            place = slice(i * tok_piece, (i + 1) * tok_piece)
            for o in range(n_own):
                spread[o * rank : (o + 1) * rank, place] = (
                    value * choose_ref[o : o + 1, place]
                ).astype(jnp.bfloat16)

        def step(i, _):
            place = lanes(i * TILE, TILE)
            piece_a[:, place] = jnp.dot(
                spread[...], hid[:, place], preferred_element_type=jnp.float32
            ).astype(jnp.bfloat16)
            return 0

        lax.fori_loop(0, ff_half // TILE, step, 0)
        return_a(True)
        spread_own[...] = jnp.transpose(
            spread[:, lanes(at_t * half, half)].astype(jnp.float32)
        ).astype(jnp.bfloat16)

    ratio = n_adapter // n_pair
    core = lax.div(at_a, ratio)
    low_a = lax.rem(at_a, ratio)
    ret_slot = (low_a * n_data + at_d) * n_pair + at_t
    ret_place = lanes(low_a * ff + at_t * ff_half, ff_half)

    def return_copy(k):
        o = lax.rem(at_own + k, n_own)
        return remote(
            piece_a.at[rows(o * rank, rank), :],
            back_a.at[at_d, :, ret_place],
            ra_send.at[k],
            ra_recv.at[ret_slot],
            dev(lax.div(o, n_data), lax.rem(o, n_data), core),
        )

    def return_a(start):
        for k in far_first:
            if start:
                return_copy(k).start()
            else:
                return_copy(k).wait_send()

        @pl.when(at_t != core)
        def _():
            if start:
                return_copy(0).start()
            else:
                return_copy(0).wait_send()

        if start:

            @pl.when(at_t == core)
            def _():
                pltpu.make_async_copy(
                    piece_a.at[rows(at_own * rank, rank), :],
                    back_a.at[at_d, :, ret_place],
                    ra_recv.at[ret_slot],
                ).start()

    def wait_returned():
        for s in range(ratio * n_data * n_pair):
            a2, d2, t2 = s // (n_data * n_pair), s // n_pair % n_data, s % n_pair
            first = a2 * ff + t2 * ff_half
            place = back_a.at[d2, :, first : first + ff_half]
            remote(place, place, ra_send.at[0], ra_recv.at[s], pair_dev).wait_recv()

    def return_b():
        copies = []
        for k in range(1, n_data):
            j = lax.rem(at_d + k, n_data)
            copies.append(
                remote(
                    piece_b.at[j], back_b.at[at_d], rb_send.at[k], rb_recv.at[k], dev(at_a, j, at_t)
                )
            )
        return copies

    def use_u():
        parts = []
        for i in range(n_sum):
            value = low[i, 0].astype(jnp.float32) * adapter_scale
            place = slice(i * tok_piece, (i + 1) * tok_piece)
            parts.append(
                jnp.concatenate(
                    [
                        value * choose_mine_ref[j : j + 1, place]
                        for j in range(n_data)
                    ],
                    axis=0,
                ).astype(jnp.bfloat16)
            )
        spread_u = jnp.concatenate(parts, axis=1)
        back_b[at_d] = jnp.zeros_like(back_b[0])
        for i in range(width // 512):
            place = slice(i * 512, (i + 1) * 512)
            wide = jnp.dot(spread_u, grad[:, place], preferred_element_type=jnp.float32)
            for j in range(n_data):
                piece_b[j, :, place] = wide[j * rank : (j + 1) * rank]
        start_all(return_b())

    events = {3: part_v, 5: part_u, 7: sum_low, 9: use_v, 10: use_u}

    def main(c, _):
        load_weight(c).wait()
        w = weight[pl.ds(pl.multiple_of(c * TILE, TILE), TILE), :]
        both = lax.dot_general(grad[...], w, NT, preferred_element_type=jnp.float32)
        to_pair[c] = jnp.where(at_t == 0, both[half:], both[:half]).astype(jnp.bfloat16)
        own_acc[c] = jnp.where(at_t == 0, both[:half], both[half:])
        pair_copy(c).start()
        for at, event in events.items():
            pl.when(c == min(at, n_tile - 1))(event)
        return 0

    lax.fori_loop(0, n_tile, main, 0)
    forward.wait()

    def store_copy(c):
        return pltpu.make_async_copy(staged.at[c], out_hbm.at[:, lanes(c * TILE, TILE)], out_sem.at[c])

    def finish(c, _):
        pair_copy(c).wait()
        total = own_acc[c] + from_pair[c].astype(jnp.float32)
        total += jnp.dot(
            spread_own[...], panels_a[:, lanes(c * TILE, TILE)], preferred_element_type=jnp.float32
        )
        for i in range(TILE // 128):
            place = slice(i * 128, (i + 1) * 128)
            staged[c, :, place] = jnp.where(live_ref[...] > 0, total[:, place], 0.0).astype(
                jnp.bfloat16
            )
        store_copy(c).start()
        return 0

    lax.fori_loop(0, n_tile, finish, 0)

    wait_all(return_b())
    for l in range(n_slot):
        total = jnp.zeros_like(piece_b[0])
        for d in range(n_data):
            from_here = jnp.where(at_d == d, 1.0, 0.0) * pick[d][l]
            total += piece_b[d] * from_here
            total += back_b[d] * (pick[d][l] - from_here)
        grad_b_ref[l] = total
    return_a(False)
    wait_returned()
    for l in range(n_slot):
        total = back_a[0].astype(jnp.float32) * pick[0][l]
        for d in range(1, n_data):
            total += back_a[d].astype(jnp.float32) * pick[d][l]
        grad_a_ref[l] = total

    def drain(c, _):
        store_copy(c).wait()
        return 0

    lax.fori_loop(0, n_tile, drain, 0)


def fused_on_device(
    output_gradient,
    hidden,
    frozen_down_weight,
    adapter_input_panels,
    adapter_output_panels,
    token_adapter_table,
    adapter_slot_table,
    segment_live_tokens,
):
    tok, width = output_gradient.shape
    ff = hidden.shape[1]
    n_slot, rank, ff_all = adapter_input_panels.shape
    n_adapter = lax.axis_size("adapter")
    n_data = lax.axis_size("dp")
    n_pair = lax.axis_size("tensor")
    n_own = n_adapter * n_data
    n_sum = n_adapter * n_pair
    half = tok // n_pair
    ff_half = ff // n_pair
    n_tile = ff // TILE
    anywhere = pl.BlockSpec(memory_space=pl.ANY)
    vmem = pl.BlockSpec(memory_space=pltpu.VMEM)
    smem = pl.BlockSpec(memory_space=pltpu.SMEM)
    dma = pltpu.SemaphoreType.DMA
    bf16, f32 = jnp.bfloat16, jnp.float32
    ff_out = ff_all // n_pair
    n_back = n_adapter // n_pair * n_data * n_pair
    outs = pl.pallas_call(
        functools.partial(fused_kernel, (n_adapter, n_data, n_pair, rank)),
        out_shape=(
            jax.ShapeDtypeStruct((half, ff), bf16),
            jax.ShapeDtypeStruct((n_slot, rank, ff_out), f32),
            jax.ShapeDtypeStruct((n_slot, rank, width), f32),
        ),
        in_specs=[anywhere] * 5 + [vmem, smem, smem],
        out_specs=(anywhere, vmem, vmem),
        scratch_shapes=[
            pltpu.VMEM((tok, width), bf16),
            pltpu.VMEM((tok, ff_half), bf16),
            pltpu.VMEM((ff, width), bf16),
            pltpu.VMEM((n_slot, rank, ff_all), bf16),
            pltpu.VMEM((n_slot, rank, width), bf16),
            pltpu.VMEM((n_data, rank, ff_all), bf16),
            pltpu.VMEM((n_data, rank, width), bf16),
            pltpu.VMEM((n_own, tok), f32),
            pltpu.VMEM((n_data, tok), f32),
            pltpu.VMEM((half, 128), f32),
            pltpu.VMEM((n_own * rank, ff), bf16),
            pltpu.VMEM((n_data * rank, width), bf16),
            pltpu.VMEM((n_tile, half, TILE), f32),
            pltpu.VMEM((n_tile, half, TILE), bf16),
            pltpu.VMEM((n_tile, half, TILE), bf16),
            pltpu.VMEM((n_tile, half, TILE), bf16),
            pltpu.VMEM((n_sum, 2, rank, tok // n_sum), f32),
            pltpu.VMEM((n_sum, 2, rank, tok // n_sum), f32),
            pltpu.VMEM((n_sum, 2, rank, tok // n_sum), bf16),
            pltpu.VMEM((n_own * rank, tok), bf16),
            pltpu.VMEM((half, n_own * rank), bf16),
            pltpu.VMEM((n_own * rank, ff_half), bf16),
            pltpu.VMEM((n_data, rank, ff_out), bf16),
            pltpu.VMEM((n_data, rank, width), f32),
            pltpu.VMEM((n_data, rank, width), f32),
            dma((6,)),
            dma((n_tile,)),
            dma((n_tile,)),
            dma((n_own,)),
            dma((n_own,)),
            dma((n_data,)),
            dma((n_data,)),
            dma((n_tile,)),
            dma((n_tile,)),
            dma((2,)),
            dma((n_sum,)),
            dma((n_sum,)),
            dma((n_sum,)),
            dma((n_sum,)),
            dma((n_own,)),
            dma((n_back,)),
            dma((n_data,)),
            dma((n_data,)),
        ],
        compiler_params=pltpu.CompilerParams(
            collective_id=0, has_side_effects=True, vmem_limit_bytes=60 * 1024 * 1024
        ),
        cost_estimate=pl.CostEstimate(
            flops=2 * tok * width * ff, bytes_accessed=2 * ff * width, transcendentals=0
        ),
    )(
        output_gradient,
        hidden,
        frozen_down_weight,
        adapter_input_panels,
        adapter_output_panels,
        token_adapter_table.reshape(n_data, 1, tok),
        adapter_slot_table,
        segment_live_tokens,
    )
    return tuple(copy_out(outs))


def copy_kernel(n_arrays, n_cuts, *refs):
    held = refs[2 * n_arrays : 3 * n_arrays]
    in_sem, out_sem = refs[3 * n_arrays :]
    loads, stores = [], []
    for a in range(n_arrays):
        src, dst = refs[a], refs[n_arrays + a]
        rows = src.shape[0] // n_cuts[a]
        for i in range(n_cuts[a]):
            place, at = slice(i * rows, (i + 1) * rows), len(loads)
            loads.append(
                pltpu.make_async_copy(src.at[place], held[a].at[place], in_sem.at[at])
            )
            stores.append(
                pltpu.make_async_copy(held[a].at[place], dst.at[place], out_sem.at[at])
            )
    for load in loads:
        load.start()
    for load, store in zip(loads, stores):
        load.wait()
        store.start()
    for store in stores:
        store.wait()


def copy_out(arrays):
    anywhere = pl.BlockSpec(memory_space=pl.ANY)
    cuts = [8 if array.ndim == 2 else array.shape[0] for array in arrays]
    size = sum(array.size * array.dtype.itemsize for array in arrays)
    return pl.pallas_call(
        functools.partial(copy_kernel, len(arrays), cuts),
        out_shape=[jax.ShapeDtypeStruct(array.shape, array.dtype) for array in arrays],
        in_specs=[anywhere] * len(arrays),
        out_specs=[anywhere] * len(arrays),
        scratch_shapes=[pltpu.VMEM(array.shape, array.dtype) for array in arrays]
        + [pltpu.SemaphoreType.DMA((sum(cuts),))] * 2,
        compiler_params=pltpu.CompilerParams(vmem_limit_bytes=60 * 1024 * 1024),
        cost_estimate=pl.CostEstimate(flops=0, bytes_accessed=2 * size, transcendentals=0),
    )(*arrays)


def fits_kernel(hidden, adapter_input_panels):
    ff = hidden.shape[1]
    n_slot, rank, _ = adapter_input_panels.shape
    n_adapter = lax.axis_size("adapter")
    n_data = lax.axis_size("dp")
    n_pair = lax.axis_size("tensor")
    n_sum = n_adapter * n_pair
    return (
        n_pair == 2
        and n_slot == 2
        and rank == 16
        and n_adapter % n_pair == 0
        and ff % (n_pair * TILE) == 0
        and ff // TILE > 11
        and hidden.shape[0] == n_sum * 128
        and n_adapter * n_data * rank <= 256
        and adapter_input_panels.shape[2] % 512 == 0
    )


def on_device(*args):
    if fits_kernel(args[1], args[3]):
        return fused_on_device(*args)
    return plain_on_device(*args)


def solution(mesh):
    placed = (
        P(("groups", "dp"), "tensor"),
        P(("groups", "dp"), "adapter"),
        P("adapter", "tensor"),
        P(("groups", "adapter", "dp"), None, None),
        P(("groups", "adapter", "dp"), None, "tensor"),
        P("groups"),
        P("groups"),
        P(("groups", "dp")),
    )
    return jax.shard_map(
        on_device,
        mesh=mesh,
        in_specs=placed,
        out_specs=(
            P(("groups", "dp", "tensor"), "adapter"),
            P(("groups", "adapter", "dp"), None, "tensor"),
            P(("groups", "adapter", "dp"), None, "tensor"),
        ),
        check_vma=False,
    )
```

```python
import functools

import jax
import jax.numpy as jnp
from jax import lax
from jax.experimental import pallas as pl
from jax.experimental.pallas import tpu as pltpu
from jax.sharding import PartitionSpec as P

adapter_scale = 4.0
MESH = pl.DeviceIdType.MESH
NT = (((1,), (1,)), ((), ()))
TILE = 256


def lookup(keys_row, table):
    positions = jnp.arange(table.shape[0], dtype=jnp.int32)
    picked = jnp.where(keys_row[:, None] == positions[None, :], table[None, :], 0)
    return jnp.sum(picked, axis=1)


def plain_on_device(
    output_gradient,
    hidden,
    frozen_down_weight,
    adapter_input_panels,
    adapter_output_panels,
    token_adapter_table,
    adapter_slot_table,
    segment_live_tokens,
):
    tok_rows = output_gradient.shape[0]
    half_width = output_gradient.shape[1]
    ff_share = hidden.shape[1]
    owned_slot_list = adapter_input_panels.shape[0]
    rank_extent = adapter_input_panels.shape[1]
    n_adapter = lax.axis_size("adapter")
    n_data = lax.axis_size("dp")
    n_pair = lax.axis_size("tensor")
    capacity = owned_slot_list // 2
    owners = n_adapter * n_data
    n_slots = owners * owned_slot_list
    d_piece = half_width // n_adapter
    ff_piece = ff_share // n_pair
    half_rows = tok_rows // n_pair
    n_recv = owners * capacity
    segment_rows = tok_rows // segment_live_tokens.shape[0]
    at_adapter = lax.axis_index("adapter")
    at_data = lax.axis_index("dp")
    at_pair = lax.axis_index("tensor")
    at_owner = at_adapter * n_data + at_data
    slot_ids = jnp.arange(n_slots, dtype=jnp.int32)
    token_slot = lookup(token_adapter_table, adapter_slot_table).reshape(n_data, tok_rows)
    used_flags = jnp.any(token_slot[:, :, None] == slot_ids[None, None, :], axis=1).astype(
        jnp.int32
    )
    used_blocks = used_flags.reshape(n_data, owners, owned_slot_list)
    order_in_block = jnp.cumsum(used_blocks, axis=2) - 1
    mine_used = lax.dynamic_index_in_dim(used_blocks, at_owner, 1, False)
    mine_order = lax.dynamic_index_in_dim(order_in_block, at_owner, 1, False)
    cap_ids = jnp.arange(capacity, dtype=jnp.int32)
    picks = (mine_used[:, None, :] == 1) & (mine_order[:, None, :] == cap_ids[None, :, None])
    lower_selection = picks.astype(jnp.bfloat16)
    picks_full = picks.astype(jnp.float32)
    sent_a = jnp.einsum(
        "mjt,tou->mjou", lower_selection, adapter_input_panels, preferred_element_type=jnp.float32
    ).astype(jnp.bfloat16)
    sent_b = jnp.einsum(
        "tke,eop->tkop", lower_selection, adapter_output_panels, preferred_element_type=jnp.float32
    ).astype(jnp.bfloat16)
    sent_a = sent_a.reshape(n_data, capacity, rank_extent, n_adapter, ff_share).transpose(
        3, 0, 1, 2, 4
    )
    sent_b = sent_b.reshape(n_data, capacity, rank_extent, n_adapter, d_piece).transpose(
        3, 0, 1, 2, 4
    )
    flat_a = sent_a.reshape(n_recv, rank_extent, ff_share)
    flat_b = sent_b.reshape(n_recv, rank_extent, d_piece)
    got_a, got_b = (
        lax.all_to_all(flat_a, ("adapter", "dp"), split_axis=0, concat_axis=0, tiled=True),
        lax.all_to_all(flat_b, ("adapter", "dp"), split_axis=0, concat_axis=0, tiled=True),
    )
    panels_a = got_a.reshape(n_recv * rank_extent, ff_share)
    panels_b = got_b.reshape(n_recv * rank_extent, d_piece)
    my_slots = lax.dynamic_index_in_dim(token_slot, at_data, 0, False)
    my_order = lax.dynamic_index_in_dim(order_in_block, at_data, 0, False).reshape(n_slots)
    recv_index = my_slots // owned_slot_list * capacity + lookup(my_slots, my_order)
    recv_ids = jnp.arange(n_recv, dtype=jnp.int32)
    select = (recv_index[:, None] == recv_ids[None, :])[:, :, None]
    seg_pos = jnp.arange(segment_rows, dtype=jnp.int32)
    live_mask = (seg_pos[None, :] < segment_live_tokens[:, None]).reshape(tok_rows)
    live_grad = jnp.where(live_mask[:, None], output_gradient, jnp.zeros_like(output_gradient))
    hidden_part = lax.dynamic_slice_in_dim(hidden, at_pair * ff_piece, ff_piece, 1)
    panels_part = lax.dynamic_slice_in_dim(panels_a, at_pair * ff_piece, ff_piece, 1)
    grad_piece = lax.dynamic_slice_in_dim(live_grad, at_adapter * d_piece, d_piece, 1)
    wide_u = jnp.einsum("tf,kf->tk", hidden_part, panels_part, preferred_element_type=jnp.float32)
    wide_v = jnp.einsum("td,kd->tk", grad_piece, panels_b, preferred_element_type=jnp.float32)
    part_u = jnp.sum(jnp.where(select, wide_u.reshape(tok_rows, n_recv, rank_extent), 0.0), axis=1)
    part_v = jnp.sum(jnp.where(select, wide_v.reshape(tok_rows, n_recv, rank_extent), 0.0), axis=1)
    full_u, full_v = lax.psum((part_u, part_v), ("adapter", "tensor"))
    first_round_result = full_u.astype(jnp.bfloat16)
    second_round_result = full_v.astype(jnp.bfloat16)
    zero_low = jnp.zeros((), jnp.bfloat16)
    spread_u = jnp.where(select, first_round_result[:, None, :], zero_low).reshape(
        tok_rows, n_recv * rank_extent
    )
    spread_v = jnp.where(select, second_round_result[:, None, :], zero_low).reshape(
        tok_rows, n_recv * rank_extent
    )
    frozen_portion = lax.psum_scatter(
        jnp.einsum("td,fd->tf", live_grad, frozen_down_weight, preferred_element_type=jnp.float32),
        "tensor",
        scatter_dimension=0,
        tiled=True,
    )
    spread_half = lax.dynamic_slice_in_dim(spread_v, at_pair * half_rows, half_rows, 0)
    hidden_half = lax.dynamic_slice_in_dim(hidden, at_pair * half_rows, half_rows, 0)
    adapter_token_rows = jnp.dot(spread_half, panels_a, preferred_element_type=jnp.float32)
    hidden_gradient = (frozen_portion + adapter_scale * adapter_token_rows).astype(jnp.bfloat16)
    input_portion = adapter_scale * jnp.einsum(
        "tk,tf->kf", spread_half, hidden_half, preferred_element_type=jnp.float32
    )
    output_portion = adapter_scale * jnp.einsum(
        "tk,td->kd", spread_u, grad_piece, preferred_element_type=jnp.float32
    )
    a_width = input_portion.shape[1]
    back_a = input_portion.reshape(n_adapter, n_data, capacity, rank_extent, a_width)
    back_b = output_portion.reshape(n_adapter, n_data, capacity, rank_extent, d_piece)
    flat_back_a = back_a.reshape(n_recv, rank_extent, a_width)
    flat_back_b = back_b.reshape(n_recv, rank_extent, d_piece)
    ret_a, ret_b = (
        lax.all_to_all(flat_back_a, ("adapter", "dp"), split_axis=0, concat_axis=0, tiled=True),
        lax.all_to_all(flat_back_b, ("adapter", "dp"), split_axis=0, concat_axis=0, tiled=True),
    )
    ret_a = ret_a.reshape(n_adapter, n_data, capacity, rank_extent, a_width)
    ret_b = ret_b.reshape(n_adapter, n_data, capacity, rank_extent, d_piece)
    own_a = jnp.einsum("jcl,kjcrf->lrkf", picks_full, ret_a, precision=lax.Precision.HIGHEST)
    own_b = jnp.einsum("jcl,kjcrd->lrkd", picks_full, ret_b, precision=lax.Precision.HIGHEST)
    own_b = own_b.reshape(owned_slot_list, rank_extent, half_width)
    own_a = own_a.reshape(owned_slot_list, rank_extent, n_adapter * a_width)
    grad_a = lax.psum_scatter(own_a, "tensor", scatter_dimension=2, tiled=True)
    return (hidden_gradient, grad_a, own_b)


def fused_kernel(
    sizes,
    grad_hbm,
    hidden_hbm,
    weight_hbm,
    slots_a_hbm,
    slots_b_hbm,
    ids_ref,
    table_ref,
    seg_ref,
    out_hbm,
    grad_a_ref,
    grad_b_ref,
    grad,
    hid,
    weight,
    slots_a,
    slots_b,
    sent_a,
    sent_b,
    choose_ref,
    choose_mine_ref,
    live_ref,
    panels_a,
    panels_b,
    own_acc,
    to_pair,
    from_pair,
    staged,
    part,
    part_in,
    low,
    spread,
    spread_own,
    piece_a,
    back_a,
    piece_b,
    back_b,
    load_sem,
    weight_sem,
    out_sem,
    a_send,
    a_recv,
    b_send,
    b_recv,
    pair_send,
    pair_recv,
    fwd_sem,
    rs_send,
    rs_recv,
    ag_send,
    ag_recv,
    ra_send,
    ra_recv,
    rb_send,
    rb_recv,
):
    n_adapter, n_data, n_pair, rank = sizes
    tok, width = grad.shape
    half = tok // n_pair
    ff_half = hid.shape[1]
    ff = ff_half * n_pair
    n_own = n_adapter * n_data
    n_sum = n_adapter * n_pair
    tok_piece = tok // n_sum
    n_tile = ff // TILE
    at_g = lax.axis_index("groups")
    at_a = lax.axis_index("adapter")
    at_d = lax.axis_index("dp")
    at_t = lax.axis_index("tensor")
    at_own = at_a * n_data + at_d
    at_sum = at_a * n_pair + at_t

    def dev(a, d, t):
        return (at_g, a, d, t)

    far_first = sorted(range(1, n_own), key=lambda k: -min(k, n_own - k))

    def remote(src, dst, send, recv, to):
        return pltpu.make_async_remote_copy(
            src_ref=src, dst_ref=dst, send_sem=send, recv_sem=recv, device_id=to, device_id_type=MESH
        )

    def lanes(start, size):
        return pl.ds(pl.multiple_of(start, 128), size)

    def rows(start, size):
        return pl.ds(pl.multiple_of(start, 16), size)

    load_grad = pltpu.make_async_copy(grad_hbm, grad, load_sem.at[0])
    load_hid = pltpu.make_async_copy(
        hidden_hbm.at[:, lanes(at_t * ff_half, ff_half)], hid, load_sem.at[1]
    )
    load_slots_a = pltpu.make_async_copy(slots_a_hbm, slots_a, load_sem.at[4])
    load_slots_b = pltpu.make_async_copy(slots_b_hbm, slots_b, load_sem.at[5])
    load_slots_b.start()
    load_slots_a.start()
    load_grad.start()

    def load_weight(c):
        place = pl.ds(pl.multiple_of(c * TILE, TILE), TILE)
        return pltpu.make_async_copy(weight_hbm.at[place, :], weight.at[place, :], weight_sem.at[c])

    def start_weight(c, _):
        load_weight(c).start()
        return 0

    load_weight(0).start()
    load_weight(1).start()

    at_all = at_own * n_pair + at_t
    n_all = n_own * n_pair
    barrier = pltpu.get_barrier_semaphore()

    def greet(k, _):
        i = lax.rem(at_all + k, n_all)
        pl.semaphore_signal(
            barrier,
            inc=1,
            device_id=dev(
                lax.div(i, n_data * n_pair), lax.rem(lax.div(i, n_pair), n_data), lax.rem(i, n_pair)
            ),
            device_id_type=MESH,
        )
        return 0

    lax.fori_loop(1, n_all, greet, 0)

    n_slot = slots_a.shape[0]
    seg = tok // seg_ref.shape[0]

    def slots_of(d):
        ids = ids_ref[d]
        slots = jnp.zeros_like(ids)
        for i in range(table_ref.shape[0]):
            slots = jnp.where(ids == i, table_ref[i], slots)
        return slots

    pick = [
        [
            jnp.max(
                jnp.where(slots_of(d) == at_own * n_slot + l, 1.0, 0.0), axis=1, keepdims=True
            )
            for l in range(n_slot)
        ]
        for d in range(n_data)
    ]
    def choose_slots(slots, sent, size):
        def step(i, _):
            place = lanes(i * size, size)
            for d in range(n_data):
                total = slots[0, :, place].astype(jnp.float32) * pick[d][0]
                for l in range(1, n_slot):
                    total += slots[l, :, place].astype(jnp.float32) * pick[d][l]
                sent[d, :, place] = total.astype(jnp.bfloat16)
            return 0

        lax.fori_loop(0, slots.shape[2] // size, step, 0)

    pl.semaphore_wait(barrier, n_all - 1)
    load_slots_b.wait()
    choose_slots(slots_b, sent_b, 512)
    b_copies = [
        pltpu.make_async_copy(
            sent_b.at[at_d], panels_b.at[rows(at_d * rank, rank), :], load_sem.at[2]
        )
    ]
    for k in range(1, n_data):
        j = lax.rem(at_d + k, n_data)
        b_copies.append(
            remote(
                sent_b.at[j],
                panels_b.at[rows(at_d * rank, rank), :],
                b_send.at[k],
                b_recv.at[k],
                dev(at_a, j, at_t),
            )
        )
    for copy in b_copies:
        copy.start()

    load_slots_a.wait()
    choose_slots(slots_a, sent_a, ff_half)

    mine = lanes(at_t * ff_half, ff_half)
    a_copies = [
        pltpu.make_async_copy(
            sent_a.at[at_d, :, lanes(at_a * ff + at_t * ff_half, ff_half)],
            panels_a.at[rows(at_own * rank, rank), mine],
            load_sem.at[3],
        )
    ]
    for k in far_first:
        o = lax.rem(at_own + k, n_own)
        a2, d2 = lax.div(o, n_data), lax.rem(o, n_data)
        a_copies.append(
            remote(
                sent_a.at[d2, :, lanes(a2 * ff + at_t * ff_half, ff_half)],
                panels_a.at[rows(at_own * rank, rank), mine],
                a_send.at[k],
                a_recv.at[k],
                dev(a2, d2, at_t),
            )
        )
    for copy in a_copies:
        copy.start()
    lax.fori_loop(2, 6, start_weight, 0)
    load_hid.start()
    lax.fori_loop(6, n_tile, start_weight, 0)
    load_grad.wait()

    spot = lax.broadcasted_iota(jnp.int32, (1, tok), 1)
    limit = jnp.zeros((1, tok), jnp.int32)
    for i in range(tok // seg):
        limit = jnp.where(spot >= i * seg, seg_ref[i] + i * seg, limit)
    my_owner = lax.shift_right_logical(slots_of(at_d), 1)
    my_owner = jnp.where(spot < limit, my_owner, n_own)
    owner_ids = lax.broadcasted_iota(jnp.int32, (n_own, tok), 0)
    choose_ref[...] = jnp.where(owner_ids == my_owner, 1.0, 0.0)
    data_ids = lax.broadcasted_iota(jnp.int32, (n_data, tok), 0)
    choose_mine_ref[...] = jnp.where(data_ids + at_a * n_data == my_owner, 1.0, 0.0)
    row_in_seg = lax.broadcasted_iota(jnp.int32, (seg, 128), 0)
    for i in range(half // seg):
        live = seg_ref[at_t * (half // seg) + i]
        live_ref[i * seg : (i + 1) * seg, :] = jnp.where(row_in_seg < live, 1.0, 0.0)


    pair_dev = dev(at_a, at_d, 1 - at_t)

    def pair_copy(c):
        return remote(to_pair.at[c], from_pair.at[c], pair_send.at[c], pair_recv.at[c], pair_dev)

    forward = remote(
        panels_a.at[:, mine], panels_a.at[:, mine], fwd_sem.at[0], fwd_sem.at[1], pair_dev
    )

    def sum_peer(k):
        q = lax.rem(at_sum + k, n_sum)
        return q, dev(lax.div(q, n_pair), at_d, lax.rem(q, n_pair))

    def scatter_copies():
        copies = []
        for k in range(1, n_sum):
            q, to = sum_peer(k)
            copies.append(
                remote(
                    part.at[q], part_in.at[k], rs_send.at[k], rs_recv.at[k], to
                )
            )
        return copies

    def gather_copies():
        copies = []
        for k in range(1, n_sum):
            _, to = sum_peer(k)
            copies.append(
                remote(
                    low.at[at_sum], low.at[at_sum], ag_send.at[k], ag_recv.at[k], to
                )
            )
        return copies

    def start_all(copies):
        for copy in copies:
            copy.start()

    def wait_all(copies):
        for copy in copies:
            copy.wait()

    def store_part(w, i, value):
        for s in range(TILE // tok_piece):
            part[i * (TILE // tok_piece) + s, w] = value[:, s * tok_piece : (s + 1) * tok_piece]

    def part_v():
        wait_all(b_copies)

        def step(i, _):
            block = grad[pl.ds(pl.multiple_of(i * TILE, TILE), TILE), :]
            wide = lax.dot_general(panels_b[...], block, NT, preferred_element_type=jnp.float32)
            total = jnp.zeros((rank, TILE), jnp.float32)
            for j in range(n_data):
                keep = choose_mine_ref[j : j + 1, lanes(i * TILE, TILE)]
                total += wide[j * rank : (j + 1) * rank] * keep
            store_part(1, i, total)
            return 0

        lax.fori_loop(0, tok // TILE, step, 0)

    def part_u():
        wait_all(a_copies)
        load_hid.wait()
        forward.start()

        def step(i, _):
            block = hid[pl.ds(pl.multiple_of(i * TILE, TILE), TILE), :]
            wide = lax.dot_general(
                panels_a[:, mine], block, NT, preferred_element_type=jnp.float32
            )
            total = jnp.zeros((rank, TILE), jnp.float32)
            for o in range(n_own):
                keep = choose_ref[o : o + 1, lanes(i * TILE, TILE)]
                total += wide[o * rank : (o + 1) * rank] * keep
            store_part(0, i, total)
            return 0

        lax.fori_loop(0, tok // TILE, step, 0)
        start_all(scatter_copies())

    def sum_low():
        wait_all(scatter_copies())
        total = part[at_sum]
        for k in range(1, n_sum):
            total += part_in[k]
        low[at_sum] = total.astype(jnp.bfloat16)
        start_all(gather_copies())

    def use_v():
        wait_all(gather_copies())
        for i in range(n_sum):
            value = low[i, 1].astype(jnp.float32) * adapter_scale
            place = slice(i * tok_piece, (i + 1) * tok_piece)
            for o in range(n_own):
                spread[o * rank : (o + 1) * rank, place] = (
                    value * choose_ref[o : o + 1, place]
                ).astype(jnp.bfloat16)

        def step(i, _):
            place = lanes(i * TILE, TILE)
            piece_a[:, place] = jnp.dot(
                spread[...], hid[:, place], preferred_element_type=jnp.float32
            ).astype(jnp.bfloat16)
            return 0

        lax.fori_loop(0, ff_half // TILE, step, 0)
        return_a(True)
        spread_own[...] = jnp.transpose(
            spread[:, lanes(at_t * half, half)].astype(jnp.float32)
        ).astype(jnp.bfloat16)

    ratio = n_adapter // n_pair
    core = lax.div(at_a, ratio)
    low_a = lax.rem(at_a, ratio)
    ret_slot = (low_a * n_data + at_d) * n_pair + at_t
    ret_place = lanes(low_a * ff + at_t * ff_half, ff_half)

    def return_copy(k):
        o = lax.rem(at_own + k, n_own)
        return remote(
            piece_a.at[rows(o * rank, rank), :],
            back_a.at[at_d, :, ret_place],
            ra_send.at[k],
            ra_recv.at[ret_slot],
            dev(lax.div(o, n_data), lax.rem(o, n_data), core),
        )

    def return_a(start):
        for k in far_first:
            if start:
                return_copy(k).start()
            else:
                return_copy(k).wait_send()

        @pl.when(at_t != core)
        def _():
            if start:
                return_copy(0).start()
            else:
                return_copy(0).wait_send()

        if start:

            @pl.when(at_t == core)
            def _():
                pltpu.make_async_copy(
                    piece_a.at[rows(at_own * rank, rank), :],
                    back_a.at[at_d, :, ret_place],
                    ra_recv.at[ret_slot],
                ).start()

    def wait_returned():
        for s in range(ratio * n_data * n_pair):
            a2, d2, t2 = s // (n_data * n_pair), s // n_pair % n_data, s % n_pair
            first = a2 * ff + t2 * ff_half
            place = back_a.at[d2, :, first : first + ff_half]
            remote(place, place, ra_send.at[0], ra_recv.at[s], pair_dev).wait_recv()

    def return_b():
        copies = []
        for k in range(1, n_data):
            j = lax.rem(at_d + k, n_data)
            copies.append(
                remote(
                    piece_b.at[j], back_b.at[at_d], rb_send.at[k], rb_recv.at[k], dev(at_a, j, at_t)
                )
            )
        return copies

    def use_u():
        parts = []
        for i in range(n_sum):
            value = low[i, 0].astype(jnp.float32) * adapter_scale
            place = slice(i * tok_piece, (i + 1) * tok_piece)
            parts.append(
                jnp.concatenate(
                    [
                        value * choose_mine_ref[j : j + 1, place]
                        for j in range(n_data)
                    ],
                    axis=0,
                ).astype(jnp.bfloat16)
            )
        spread_u = jnp.concatenate(parts, axis=1)
        back_b[at_d] = jnp.zeros_like(back_b[0])
        for i in range(width // 512):
            place = slice(i * 512, (i + 1) * 512)
            wide = jnp.dot(spread_u, grad[:, place], preferred_element_type=jnp.float32)
            for j in range(n_data):
                piece_b[j, :, place] = wide[j * rank : (j + 1) * rank]
        start_all(return_b())

    events = {3: part_v, 5: part_u, 7: sum_low, 9: use_v, 10: use_u}

    def main(c, _):
        load_weight(c).wait()
        w = weight[pl.ds(pl.multiple_of(c * TILE, TILE), TILE), :]
        both = lax.dot_general(grad[...], w, NT, preferred_element_type=jnp.float32)
        to_pair[c] = jnp.where(at_t == 0, both[half:], both[:half]).astype(jnp.bfloat16)
        own_acc[c] = jnp.where(at_t == 0, both[:half], both[half:])
        pair_copy(c).start()
        for at, event in events.items():
            pl.when(c == min(at, n_tile - 1))(event)
        return 0

    lax.fori_loop(0, n_tile, main, 0)
    forward.wait()

    def store_copy(c):
        return pltpu.make_async_copy(staged.at[c], out_hbm.at[:, lanes(c * TILE, TILE)], out_sem.at[c])

    def finish(c, _):
        pair_copy(c).wait()
        total = own_acc[c] + from_pair[c].astype(jnp.float32)
        total += jnp.dot(
            spread_own[...], panels_a[:, lanes(c * TILE, TILE)], preferred_element_type=jnp.float32
        )
        for i in range(TILE // 128):
            place = slice(i * 128, (i + 1) * 128)
            staged[c, :, place] = jnp.where(live_ref[...] > 0, total[:, place], 0.0).astype(
                jnp.bfloat16
            )
        store_copy(c).start()
        return 0

    lax.fori_loop(0, n_tile, finish, 0)

    wait_all(return_b())
    for l in range(n_slot):
        total = jnp.zeros_like(piece_b[0])
        for d in range(n_data):
            from_here = jnp.where(at_d == d, 1.0, 0.0) * pick[d][l]
            total += piece_b[d] * from_here
            total += back_b[d] * (pick[d][l] - from_here)
        grad_b_ref[l] = total
    return_a(False)
    wait_returned()
    for l in range(n_slot):
        total = back_a[0].astype(jnp.float32) * pick[0][l]
        for d in range(1, n_data):
            total += back_a[d].astype(jnp.float32) * pick[d][l]
        grad_a_ref[l] = total

    def drain(c, _):
        store_copy(c).wait()
        return 0

    lax.fori_loop(0, n_tile, drain, 0)


def fused_on_device(
    output_gradient,
    hidden,
    frozen_down_weight,
    adapter_input_panels,
    adapter_output_panels,
    token_adapter_table,
    adapter_slot_table,
    segment_live_tokens,
):
    tok, width = output_gradient.shape
    ff = hidden.shape[1]
    n_slot, rank, ff_all = adapter_input_panels.shape
    n_adapter = lax.axis_size("adapter")
    n_data = lax.axis_size("dp")
    n_pair = lax.axis_size("tensor")
    n_own = n_adapter * n_data
    n_sum = n_adapter * n_pair
    half = tok // n_pair
    ff_half = ff // n_pair
    n_tile = ff // TILE
    anywhere = pl.BlockSpec(memory_space=pl.ANY)
    vmem = pl.BlockSpec(memory_space=pltpu.VMEM)
    smem = pl.BlockSpec(memory_space=pltpu.SMEM)
    dma = pltpu.SemaphoreType.DMA
    bf16, f32 = jnp.bfloat16, jnp.float32
    ff_out = ff_all // n_pair
    n_back = n_adapter // n_pair * n_data * n_pair
    outs = pl.pallas_call(
        functools.partial(fused_kernel, (n_adapter, n_data, n_pair, rank)),
        out_shape=(
            jax.ShapeDtypeStruct((half, ff), bf16),
            jax.ShapeDtypeStruct((n_slot, rank, ff_out), f32),
            jax.ShapeDtypeStruct((n_slot, rank, width), f32),
        ),
        in_specs=[anywhere] * 5 + [vmem, smem, smem],
        out_specs=(anywhere, vmem, vmem),
        scratch_shapes=[
            pltpu.VMEM((tok, width), bf16),
            pltpu.VMEM((tok, ff_half), bf16),
            pltpu.VMEM((ff, width), bf16),
            pltpu.VMEM((n_slot, rank, ff_all), bf16),
            pltpu.VMEM((n_slot, rank, width), bf16),
            pltpu.VMEM((n_data, rank, ff_all), bf16),
            pltpu.VMEM((n_data, rank, width), bf16),
            pltpu.VMEM((n_own, tok), f32),
            pltpu.VMEM((n_data, tok), f32),
            pltpu.VMEM((half, 128), f32),
            pltpu.VMEM((n_own * rank, ff), bf16),
            pltpu.VMEM((n_data * rank, width), bf16),
            pltpu.VMEM((n_tile, half, TILE), f32),
            pltpu.VMEM((n_tile, half, TILE), bf16),
            pltpu.VMEM((n_tile, half, TILE), bf16),
            pltpu.VMEM((n_tile, half, TILE), bf16),
            pltpu.VMEM((n_sum, 2, rank, tok // n_sum), f32),
            pltpu.VMEM((n_sum, 2, rank, tok // n_sum), f32),
            pltpu.VMEM((n_sum, 2, rank, tok // n_sum), bf16),
            pltpu.VMEM((n_own * rank, tok), bf16),
            pltpu.VMEM((half, n_own * rank), bf16),
            pltpu.VMEM((n_own * rank, ff_half), bf16),
            pltpu.VMEM((n_data, rank, ff_out), bf16),
            pltpu.VMEM((n_data, rank, width), f32),
            pltpu.VMEM((n_data, rank, width), f32),
            dma((6,)),
            dma((n_tile,)),
            dma((n_tile,)),
            dma((n_own,)),
            dma((n_own,)),
            dma((n_data,)),
            dma((n_data,)),
            dma((n_tile,)),
            dma((n_tile,)),
            dma((2,)),
            dma((n_sum,)),
            dma((n_sum,)),
            dma((n_sum,)),
            dma((n_sum,)),
            dma((n_own,)),
            dma((n_back,)),
            dma((n_data,)),
            dma((n_data,)),
        ],
        compiler_params=pltpu.CompilerParams(
            collective_id=0, has_side_effects=True, vmem_limit_bytes=60 * 1024 * 1024
        ),
        cost_estimate=pl.CostEstimate(
            flops=2 * tok * width * ff, bytes_accessed=2 * ff * width, transcendentals=0
        ),
    )(
        output_gradient,
        hidden,
        frozen_down_weight,
        adapter_input_panels,
        adapter_output_panels,
        token_adapter_table.reshape(n_data, 1, tok),
        adapter_slot_table,
        segment_live_tokens,
    )
    return tuple(copy_out(outs))


def copy_kernel(n_arrays, n_cuts, *refs):
    held = refs[2 * n_arrays : 3 * n_arrays]
    in_sem, out_sem = refs[3 * n_arrays :]
    loads, stores = [], []
    for a in range(n_arrays):
        src, dst = refs[a], refs[n_arrays + a]
        rows = src.shape[0] // n_cuts[a]
        for i in range(n_cuts[a]):
            place, at = slice(i * rows, (i + 1) * rows), len(loads)
            loads.append(
                pltpu.make_async_copy(src.at[place], held[a].at[place], in_sem.at[at])
            )
            stores.append(
                pltpu.make_async_copy(held[a].at[place], dst.at[place], out_sem.at[at])
            )
    for load in loads:
        load.start()
    for load, store in zip(loads, stores):
        load.wait()
        store.start()
    for store in stores:
        store.wait()


def copy_out(arrays):
    anywhere = pl.BlockSpec(memory_space=pl.ANY)
    cuts = [4 if array.ndim == 2 else array.shape[0] for array in arrays]
    size = sum(array.size * array.dtype.itemsize for array in arrays)
    return pl.pallas_call(
        functools.partial(copy_kernel, len(arrays), cuts),
        out_shape=[jax.ShapeDtypeStruct(array.shape, array.dtype) for array in arrays],
        in_specs=[anywhere] * len(arrays),
        out_specs=[anywhere] * len(arrays),
        scratch_shapes=[pltpu.VMEM(array.shape, array.dtype) for array in arrays]
        + [pltpu.SemaphoreType.DMA((sum(cuts),))] * 2,
        compiler_params=pltpu.CompilerParams(vmem_limit_bytes=60 * 1024 * 1024),
        cost_estimate=pl.CostEstimate(flops=0, bytes_accessed=2 * size, transcendentals=0),
    )(*arrays)


def fits_kernel(hidden, adapter_input_panels):
    ff = hidden.shape[1]
    n_slot, rank, _ = adapter_input_panels.shape
    n_adapter = lax.axis_size("adapter")
    n_data = lax.axis_size("dp")
    n_pair = lax.axis_size("tensor")
    n_sum = n_adapter * n_pair
    return (
        n_pair == 2
        and n_slot == 2
        and rank == 16
        and n_adapter % n_pair == 0
        and ff % (n_pair * TILE) == 0
        and ff // TILE > 11
        and hidden.shape[0] == n_sum * 128
        and n_adapter * n_data * rank <= 256
        and adapter_input_panels.shape[2] % 512 == 0
    )


def on_device(*args):
    if fits_kernel(args[1], args[3]):
        return fused_on_device(*args)
    return plain_on_device(*args)


def solution(mesh):
    placed = (
        P(("groups", "dp"), "tensor"),
        P(("groups", "dp"), "adapter"),
        P("adapter", "tensor"),
        P(("groups", "adapter", "dp"), None, None),
        P(("groups", "adapter", "dp"), None, "tensor"),
        P("groups"),
        P("groups"),
        P(("groups", "dp")),
    )
    return jax.shard_map(
        on_device,
        mesh=mesh,
        in_specs=placed,
        out_specs=(
            P(("groups", "dp", "tensor"), "adapter"),
            P(("groups", "adapter", "dp"), None, "tensor"),
            P(("groups", "adapter", "dp"), None, "tensor"),
        ),
        check_vma=False,
    )
```
